256 devices in a mesh: dp: 32 (over z, x_lo, core), ctx: 8 (over x_hi, y).
Axes of the slice: x: 4 (x_hi: 2, x_lo: 2; x = x_hi * 2 + x_lo), y: 4, z: 8, core: 2. Of those that a mesh axis runs over, the one named last changes fastest.
Arguments:
- tokens: bfloat16 [65536, 512], P(('dp', 'ctx')), may hold values from -24 to 24
- seq_lengths: int32 [32, 2], P('dp'), may hold values from 1 to 1920, 2048 in all within a row
- w_in: bfloat16 [512, 2048], P('dp'), may hold values from -0.25 to 0.25
- w_out: bfloat16 [512, 512], P('dp'), may hold values from -0.25 to 0.25
- cotangent: bfloat16 [65536, 512], P(('dp', 'ctx')), may hold values from -6 to 6
Outputs:
- layer_out: bfloat16 [65536, 512], P(('dp', 'ctx'))
- d_tokens: bfloat16 [65536, 512], P(('dp', 'ctx'))
- grad_in: float32 [512, 2048], P('dp')
- grad_out: float32 [512, 512], P('dp')
The draws below stay inside these ranges and needn't reach their ends.
Inputs may be any that keep to these rules, and one draw needn't show every extreme that they name: `seq_lengths`: each row lists the lengths of the 2 sequences that fill one group of 2048 positions, in order of position, and sums to 2048; its largest entry is at most 1920.
All inputs are finite; a program needn't handle non-finite values.
Results may differ from the reference program's by a relative error of at most 0.0083.
Values may be sent and summed in bfloat16 or wider, within the bound.
A program may use at most 64 MiB of HBM per device.

```python
import math
import jax
import jax.numpy as jnp
import numpy as np
from jax import lax

D = 512
HEADS = 4
TOK_DEV = 256
SEQS = 2
GROUP = 2048
LONGEST = 1920
TOKENS = 65536
N_DP = 32
N_CTX = 8


def strengthened(values, key, source, target, shards_of, factor):
    def block_of(position):
        return (jnp.arange(values.shape[position]) // (values.shape[position] // shards_of)).reshape((-1,) + (1,) * (values.ndim - 1 - position))

    first = jax.random.permutation(key, shards_of)[block_of(target)]
    second = (block_of(target) + shards_of // 2) % shards_of
    return jnp.where((block_of(source) == first) | (block_of(source) == second), factor * values, values)


def levels(stream_key, shape, shards, least, largest):
    loudness = 1.0
    for dim, parts in shards:
        heights = jax.random.uniform(jax.random.fold_in(jax.random.fold_in(stream_key, 6), dim), (parts,), jnp.float32, least / len(shards), largest / len(shards))
        loudness = loudness * jnp.repeat(jnp.exp(heights), shape[dim] // parts).reshape((-1,) + (1,) * (len(shape) - 1 - dim))
    return loudness


def length_profile(amount, total, limit, skew):
    weights = [(1 << 20) // math.isqrt(rank ** skew) + 1 for rank in range(2, amount + 1)]
    spare, holding = total - limit - (amount - 1), [1] * (amount - 1)
    while spare > 0:
        movable = [i for i in range(amount - 1) if holding[i] < limit]
        pool, budget = sum([weights[i] for i in movable]), spare
        for i in movable:
            more = min(limit - holding[i], max(1, budget * weights[i] // pool), spare)
            holding[i] = holding[i] + more
            spare = spare - more
    return np.array([limit] + holding)


def uneven(rng, number_of, total, reach, lean):
    if number_of == 2:
        one = jax.random.randint(rng, (), max(1, total - reach), min(reach, total - 1) + 1)
        return jnp.stack([one, total - one])
    sizes = jnp.asarray(length_profile(number_of, total, reach, lean), jnp.int32)
    twos = (number_of - 1) // 2
    donor, taker = sizes[1:1 + 2 * twos:2], sizes[2:2 + 2 * twos:2]
    slack = jnp.minimum(donor - 1, reach - taker)
    passed = jax.random.randint(jax.random.fold_in(rng, 1), (twos,), 0, 1 << 20) % (slack + 1)
    sizes = sizes.at[1:1 + 2 * twos:2].set(donor - passed).at[2:2 + 2 * twos:2].set(taker + passed)
    return sizes[jax.random.permutation(jax.random.fold_in(rng, 2), number_of)]


def bell_draw(key, shape, scale, bound, shards=(), held_as=jnp.bfloat16):
    result = jax.random.normal(key, shape, jnp.float32) * scale
    if len(shards) > 0:
        result = levels(key, shape, shards, -0.22, 0.18) * result
    return jnp.clip(result, min=-bound, max=bound).astype(held_as)


def heavy_noise(key, dims, scale, reach, split, heavy, kind=jnp.bfloat16):
    entries = scale * jax.random.normal(key, dims, jnp.float32)
    if split:
        entries = entries * levels(key, dims, split, -0.22, 0.18)
    return jnp.clip(strengthened(entries, jax.random.fold_in(key, 3), *heavy), -reach, reach).astype(kind)


def setup_inputs(seed: int = 0) -> dict:
    streams_of = jax.random.split(jax.random.key(seed), 6)
    return {
        "tokens": heavy_noise(streams_of[0], (TOKENS, D), 1.0, 24.0, ((0, 256),), (0, 1, 256, 6.0)),
        "seq_lengths": jax.vmap(lambda own: uneven(own, SEQS, GROUP, LONGEST, 2))(jax.random.split(streams_of[1], N_DP)).reshape((N_DP, SEQS)).astype(jnp.int32),
        "w_in": bell_draw(streams_of[2], (D, 4 * D), D ** -0.5, 0.25, ((0, 32),)),
        "w_out": bell_draw(streams_of[3], (D, D), D ** -0.5, 0.25, ((0, 32),)),
        "cotangent": bell_draw(streams_of[4], (TOKENS, D), 1.0, 6.0, ((0, 256),)),
    }


NORM_EPS = 1e-05

def norm_rows(values_in):
    centre = values_in - lax.optimization_barrier(jnp.mean(values_in, axis=-1, keepdims=True))
    spread = lax.rsqrt(lax.optimization_barrier(jnp.mean(centre * centre, axis=-1, keepdims=True)) + NORM_EPS)
    return (centre * spread, spread)

def norm_back(gradient, normed, spread):
    first_mean = lax.optimization_barrier(jnp.mean(gradient, axis=-1, keepdims=True))
    second_mean = lax.optimization_barrier(jnp.mean(gradient * normed, axis=-1, keepdims=True))
    return spread * (gradient - first_mean - normed * second_mean)

def silu_slope(values_in):
    sigmoid_v = jax.nn.sigmoid(values_in)
    return sigmoid_v * (1.0 + values_in * (1.0 - sigmoid_v))

def stored_places(stored, block_rows, cycle_count):
    half_rows = block_rows // 2
    block_id = stored // block_rows
    offset = stored % block_rows
    early = block_id * half_rows + offset
    late = (2 * cycle_count - 1 - block_id) * half_rows + offset - half_rows
    return jnp.where(offset < half_rows, early, late).astype(jnp.int32)

def group_pass(tokens, cotangent, lengths_row, w_in, w_out):
    model_width = tokens.shape[1]
    head_size = model_width // HEADS
    score_scale = 1.0 / math.sqrt(head_size)
    row_count = tokens.shape[0]
    seq_ends = jnp.cumsum(lengths_row).astype(jnp.int32)
    places = stored_places(jnp.arange(row_count, dtype=jnp.int32), TOK_DEV, N_CTX)
    labels = lax.optimization_barrier(jnp.sum((places[:, None] >= seq_ends[None, :]).astype(jnp.int32), axis=1))
    allowed = (labels[:, None] == labels[None, :]) & (places[None, :] <= places[:, None])
    x_float = tokens.astype(jnp.float32)
    x_normed, x_spread = norm_rows(x_float)
    x_normed_b = x_normed.astype(jnp.bfloat16)
    pre_act = jnp.dot(x_normed_b, w_in, preferred_element_type=jnp.float32)
    projected = jax.nn.silu(pre_act).astype(jnp.bfloat16)
    gate_float = projected[:, :model_width].astype(jnp.float32)
    query_heads = projected[:, model_width:2 * model_width].astype(jnp.float32).reshape(row_count, HEADS, head_size)
    key_heads = projected[:, 2 * model_width:3 * model_width].astype(jnp.float32).reshape(row_count, HEADS, head_size)
    value_heads = projected[:, 3 * model_width:].astype(jnp.float32).reshape(row_count, HEADS, head_size)
    scores = score_scale * jnp.einsum('ihd,jhd->hij', query_heads, key_heads)
    attn_weights = jnp.where(allowed[None], jax.nn.silu(scores), 0.0).astype(jnp.bfloat16)
    attn_float = lax.optimization_barrier(attn_weights).astype(jnp.float32)
    mixed_sum = jnp.einsum('hij,jhd->ihd', attn_float, value_heads).reshape(row_count, model_width)
    z_normed, z_spread = norm_rows(mixed_sum)
    gated_out = (z_normed * gate_float).astype(jnp.bfloat16)
    layer_out = (jnp.dot(gated_out, w_out, preferred_element_type=jnp.float32) + x_float).astype(jnp.bfloat16)
    d_gated = jnp.dot(cotangent, w_out.T, preferred_element_type=jnp.float32)
    d_z_normed = d_gated * gate_float
    d_gate = d_gated * z_normed
    d_mixed = norm_back(d_z_normed, z_normed, z_spread).astype(jnp.bfloat16)
    d_mixed_heads = lax.optimization_barrier(d_mixed).astype(jnp.float32).reshape(row_count, HEADS, head_size)
    d_value = jnp.einsum('hij,ihd->jhd', attn_float, d_mixed_heads).reshape(row_count, model_width)
    d_attn = jnp.einsum('ihd,jhd->hij', d_mixed_heads, value_heads)
    d_scores = jnp.where(allowed[None], d_attn * silu_slope(scores), 0.0).astype(jnp.bfloat16)
    d_scores_float = lax.optimization_barrier(d_scores).astype(jnp.float32)
    d_query = score_scale * jnp.einsum('hij,jhd->ihd', d_scores_float, key_heads).reshape(row_count, model_width)
    d_key = score_scale * jnp.einsum('hij,ihd->jhd', d_scores_float, query_heads).reshape(row_count, model_width)
    d_projected = jnp.concatenate([d_gate, d_query, d_key, d_value], axis=1)
    d_pre = (d_projected * silu_slope(pre_act)).astype(jnp.bfloat16)
    grad_in = jnp.dot(x_normed_b.T, d_pre, preferred_element_type=jnp.float32)
    grad_out = jnp.dot(gated_out.T, cotangent, preferred_element_type=jnp.float32)
    d_x_normed = jnp.dot(d_pre, w_in.T, preferred_element_type=jnp.float32)
    d_tokens = (norm_back(d_x_normed, x_normed, x_spread) + cotangent.astype(jnp.float32)).astype(jnp.bfloat16)
    return (layer_out, d_tokens, grad_in, grad_out)

def reference(tokens, seq_lengths, w_in, w_out, cotangent):
    token_groups = tokens.reshape(N_DP, GROUP, D)
    cotangent_groups = cotangent.reshape(N_DP, GROUP, D)

    def one_group(sums, items):
        layer_out, d_tokens, grad_in, grad_out = group_pass(items[0], items[1], items[2], w_in, w_out)
        return ((sums[0] + grad_in, sums[1] + grad_out), (layer_out, d_tokens))
    start_sums = (jnp.zeros((D, 4 * D), jnp.float32), jnp.zeros((D, D), jnp.float32))
    (grad_in, grad_out), (outs_all, grads_all) = lax.scan(one_group, start_sums, (token_groups, cotangent_groups, seq_lengths))
    return (outs_all.reshape(TOKENS, D), grads_all.reshape(TOKENS, D), grad_in, grad_out)
```

```python
import math

import jax
import jax.numpy as jnp
from jax import lax
from jax.experimental import pallas as pl
from jax.experimental.pallas import tpu as pltpu
from jax.sharding import PartitionSpec as P

MESH = pl.DeviceIdType.MESH
F32 = jnp.float32
BF16 = jnp.bfloat16
EPS = 1e-05
NZ = 8
D = 512
H = 128
SCALE = 1.0 / math.sqrt(H)
NN = (((1,), (0,)), ((), ()))
NT = (((1,), (1,)), ((), ()))
BASE = (0, 4, 7, 9)


def dot(lhs, rhs, dims=NN):
    return lax.dot_general(lhs, rhs, dims, preferred_element_type=F32)


def sigmoid(v):
    return 0.5 * jnp.tanh(0.5 * v) + 0.5


def kernel(
    tok, seq, win, wout, cot, lo_out, dt_out, gi_out, go_out,
    xa, ca, xt, w5, wo5, wgt, kv, kvt, qs, slope, gate_t, slope_gt, dg_t, dz_t,
    at, sl, mixed_t, stats, dm_t, z_t, dq_t, dkv_own, dkv_far, dkv_s, dkv_r,
    lo_f, lo_s, lo_r, dpre, dx_f, dx_s, dx_r,
    ga, gb, s1, r1, s2, r2, tot, s3, r3, fr,
    go, os1, or1, os2, or2, otot, os3, or3, ofr,
    ssem, rsem,
):
    dp = lax.axis_index("dp")
    cx = lax.axis_index("ctx")
    z, xl, k = dp // 4, (dp // 2) % 2, dp % 2
    a, y = cx // 4, cx % 4
    x = a * 2 + xl

    def at_y(s):
        return {"dp": dp, "ctx": a * 4 + (y + s) % 4}

    def at_x(s):
        there = (x + s) % 4
        return {"dp": z * 4 + (there % 2) * 2 + k, "ctx": (there // 2) * 4 + y}

    def at_z(s):
        return {"dp": ((z + s) % NZ) * 4 + xl * 2 + k, "ctx": cx}

    def at_zabs(there):
        return {"dp": there * 4 + xl * 2 + k, "ctx": cx}

    def at_ctx(s):
        return {"dp": dp, "ctx": (cx + s) % 8}

    core = {"dp": z * 4 + xl * 2 + (1 - k), "ctx": cx}
    xl_mate = {"dp": z * 4 + (1 - xl) * 2 + k, "ctx": cx}
    far = {"dp": dp, "ctx": (1 - a) * 4 + y}

    peers = [core, at_x(1), at_x(3)]
    peers += [at_z(s) for s in range(1, NZ)]
    peers += [at_ctx(s) for s in range(1, 8)]
    barrier = pltpu.get_barrier_semaphore()
    for peer in peers:
        pl.semaphore_signal(barrier, inc=1, device_id=peer, device_id_type=MESH)

    counter = [0]
    started = []

    def sems(n=1):
        first = counter[0]
        counter[0] += n
        return first

    def remote(src, dst, peer, s_index, r_index):
        return pltpu.make_async_remote_copy(
            src_ref=src, dst_ref=dst, send_sem=ssem.at[s_index], recv_sem=rsem.at[r_index],
            device_id=peer, device_id_type=MESH,
        )

    def send(src, dst, peer):
        i = sems()
        copy = remote(src, dst, peer, i, i)
        copy.start()
        started.append(copy)
        return copy

    def arrive(copies):
        for copy in copies:
            copy.wait_recv()

    early = pl.ds(pl.multiple_of(y * 128, 128), 128)
    late = pl.ds(pl.multiple_of((7 - y) * 128, 128), 128)

    def slots(s):
        there = (y + s) % 4
        return (
            pl.ds(pl.multiple_of(there * 128, 128), 128),
            pl.ds(pl.multiple_of((7 - there) * 128, 128), 128),
        )

    for part in range(4):
        w5[z, xl, k, :, part * 128 : (part + 1) * 128] = win[
            :, pl.ds(pl.multiple_of(part * D + y * 128, 128), 128)
        ]
    owner = z // 2 == y

    @pl.when(owner)
    def _():
        wo5[z % 2, xl, k] = wout[...]

    def normed(rows):
        v = tok[rows, :].astype(F32)
        centre = v - jnp.mean(v, axis=-1, keepdims=True)
        spread = lax.rsqrt(jnp.mean(centre * centre, axis=-1, keepdims=True) + EPS)
        return centre * spread, spread

    xa[early, :] = normed(pl.ds(0, 128))[0].astype(BF16)
    xa[late, :] = normed(pl.ds(128, 128))[0].astype(BF16)
    ca[early, :] = cot[0:128, :]
    ca[late, :] = cot[128:256, :]

    pl.semaphore_wait(barrier, len(peers))

    w_z = [send(w5.at[z, xl, k], w5.at[z, xl, k], at_z(s)) for s in range(1, NZ)]
    x_y = []
    for s in (1, 3, 2):
        x_y.append(send(xa.at[early], xa.at[early], at_y(s)))
        x_y.append(send(xa.at[late], xa.at[late], at_y(s)))
    wo_first = sems(NZ)

    def wo_copy(s):
        return remote(
            wo5.at[z % 2, xl, k], wo5.at[z % 2, xl, k], at_z(s), wo_first + s, wo_first + z % 2
        )

    @pl.when(owner)
    def _():
        for s in range(1, NZ):
            wo_copy(s).start()

    arrive(w_z)
    w_x = send(w5.at[:, xl, k], w5.at[:, xl, k], xl_mate)

    for j in range(2):
        @pl.when(z != 2 * y + j)
        def _():
            remote(
                wo5.at[j, xl, k], wo5.at[j, xl, k], at_z(1), wo_first, wo_first + j
            ).wait_recv()

    wo_x = send(wo5.at[:, xl, k], wo5.at[:, xl, k], xl_mate)
    arrive([w_x])
    w_k = send(w5.at[:, :, k], w5.at[:, :, k], core)
    arrive([wo_x])
    wo_k = send(wo5.at[:, :, k], wo5.at[:, :, k], core)
    arrive([w_k])
    arrive(x_y)
    c_y = []
    for s in (1, 3, 2):
        c_y.append(send(ca.at[early], ca.at[early], at_y(s)))
        c_y.append(send(ca.at[late], ca.at[late], at_y(s)))

    kv_x = []
    for i in range(4):
        rows = pl.ds(i * 256, 256)
        pre = dot(xa[rows, :], w5[:, :, :, :, 256:512].reshape(D, 256))
        sig = sigmoid(pre)
        act = pre * sig
        kv[a, rows, :] = act.astype(BF16)
        slope[rows, 128:384] = sig + act * (1.0 - sig)
        kv_x.append(send(kv.at[a, rows], kv.at[a, rows], far))
    wgt[...] = w5[:, :, :, :, 0:128].reshape(D, 128).T
    for i in range(4):
        rows = pl.ds(i * 256, 256)
        pre = dot(xa[rows, :], w5[:, :, :, :, 128:256].reshape(D, 128))
        sig = sigmoid(pre)
        act = pre * sig
        qs[rows, :] = act.astype(BF16)
        slope[rows, 0:128] = sig + act * (1.0 - sig)
        pre = dot(wgt[...], xa[rows, :], NT)
        sig = sigmoid(pre)
        act = pre * sig
        gate_t[:, rows] = act.astype(BF16).astype(F32)
        slope_gt[:, rows] = sig + act * (1.0 - sig)
        kvt[a, :, rows] = kv[a, rows, :].T
        xt[:, rows] = xa[rows, :].T

    mixed_t[...] = jnp.zeros_like(mixed_t)
    border = seq[0, 0]

    def tile(i):
        return pl.ds(pl.multiple_of(i * 256, 256), 256)

    def place(half, i):
        return i * 256 + half * 512 + (1 - half) * 1024 * (i // 2)

    def attend(half, kt, qt, index, diagonal):
        scores = dot(kv[half, tile(kt), 0:128], qs[tile(qt), :], NT)
        key_at = lax.broadcasted_iota(jnp.int32, (256, 256), 0) + place(half, kt)
        query_at = lax.broadcasted_iota(jnp.int32, (1, 256), 1) + place(a, qt)
        least = jnp.where(query_at >= border, border, 0)
        allowed = key_at >= least
        if diagonal:
            allowed = allowed & (key_at <= query_at)
        s = scores * SCALE
        sig = jnp.where(allowed, sigmoid(s), 0.0)
        act = s * sig
        act_b = act.astype(BF16)
        at[index] = act_b
        sl[index] = sig + act * (1.0 - sig)
        mixed_t[:, tile(qt)] += dot(kvt[half, 128:256, tile(kt)], act_b)

    for kt in range(4):
        attend(a, kt, kt, BASE[kt], True)
        if kt < 3:
            def step(qt, carry, kt=kt):
                attend(a, kt, qt, BASE[kt] + qt - kt, False)
                return carry

            lax.fori_loop(kt + 1, 4, step, 0)

    arrive(c_y)
    arrive([wo_k])
    for i in range(4):
        rows = pl.ds(i * 256, 256)
        part = dot(wo5[...].reshape(128, D), ca[rows, :], NT)
        dg_t[:, rows] = part
        dz_t[:, rows] = part * gate_t[:, rows]

    arrive(kv_x)
    for i in range(4):
        rows = pl.ds(i * 256, 256)
        kvt[1 - a, :, rows] = kv[1 - a, rows, :].T

    def far_tiles(t):
        return t // (2 + 2 * a), t % (2 + 2 * a) + 2 * (1 - a)

    def far_step(t, carry):
        kt, qt = far_tiles(t)
        attend(1 - a, kt, qt, 10 + t, False)
        return carry

    lax.fori_loop(0, 8, far_step, 0)

    mixed = mixed_t[...]
    mean_h = jnp.mean(mixed, axis=0, keepdims=True)
    centred = mixed - mean_h
    dz = dz_t[...]
    stats[y, 0:1, :] = mean_h
    stats[y, 1:2, :] = jnp.sum(centred * centred, axis=0, keepdims=True)
    stats[y, 2:3, :] = jnp.sum(dz, axis=0, keepdims=True)
    stats[y, 3:4, :] = jnp.sum(dz * centred, axis=0, keepdims=True)
    stats[y, 4:8, :] = jnp.zeros((4, 1024), F32)
    arrive([send(stats.at[y], stats.at[y], at_y(s)) for s in (1, 2, 3)])
    means = [stats[j, 0:1, :] for j in range(4)]
    mean = (means[0] + means[1] + means[2] + means[3]) * 0.25
    second = jnp.zeros((1, 1024), F32)
    first_dz = jnp.zeros((1, 1024), F32)
    second_dz = jnp.zeros((1, 1024), F32)
    for j in range(4):
        off = means[j] - mean
        second += stats[j, 1:2, :] + 128.0 * off * off
        first_dz += stats[j, 2:3, :]
        second_dz += stats[j, 3:4, :] + off * stats[j, 2:3, :]
    spread = lax.rsqrt(second * (1.0 / D) + EPS)
    first_dz = first_dz * (1.0 / D)
    second_dz = second_dz * (1.0 / D) * spread
    for i in range(4):
        rows = pl.ds(i * 256, 256)
        r = spread[:, i * 256 : (i + 1) * 256]
        zn = (mixed_t[:, rows] - mean[:, i * 256 : (i + 1) * 256]) * r
        z_t[:, rows] = (zn * gate_t[:, rows]).astype(BF16)
        dm_t[:, rows] = (
            r * (
                dz_t[:, rows] - first_dz[:, i * 256 : (i + 1) * 256]
                - zn * second_dz[:, i * 256 : (i + 1) * 256]
            )
        ).astype(BF16)
        dpre[rows, 0:128] = (dg_t[:, rows] * zn * slope_gt[:, rows]).astype(BF16).T

    dq_t[...] = jnp.zeros_like(dq_t)
    dkv_own[...] = jnp.zeros_like(dkv_own)
    dkv_far[...] = jnp.zeros_like(dkv_far)

    def attend_back(half, kt, qt, index, grads):
        d_attn = dot(kv[half, tile(kt), 128:256], dm_t[:, tile(qt)])
        ds = (d_attn * sl[index]).astype(BF16)
        grads[tile(kt), 128:256] += dot(at[index], dm_t[:, tile(qt)], NT)
        grads[tile(kt), 0:128] += dot(ds, qs[tile(qt), :])
        dq_t[:, tile(qt)] += dot(kvt[half, 0:128, tile(kt)], ds)

    def far_back(t, carry):
        kt, qt = far_tiles(t)
        attend_back(1 - a, kt, qt, 10 + t, dkv_far)
        return carry

    lax.fori_loop(0, 8, far_back, 0)
    dkv_x = []
    for i in range(4):
        rows = pl.ds(i * 256, 256)
        dkv_s[rows, :] = dkv_far[rows, :].astype(BF16)
        dkv_x.append(send(dkv_s.at[rows], dkv_r.at[rows], far))

    for i in range(4):
        rows = pl.ds(i * 256, 256)
        part = dot(z_t[:, rows].T, wo5[...].reshape(128, D))
        lo_f[rows, :] = part
        lo_s[rows, :] = part.astype(BF16)
    lo_y = []
    for s in (1, 3, 2):
        to_early, to_late = slots(s)
        lo_y.append(send(lo_s.at[to_early], lo_r.at[s - 1, pl.ds(0, 128)], at_y(s)))
        lo_y.append(send(lo_s.at[to_late], lo_r.at[s - 1, pl.ds(128, 128)], at_y(s)))
    go[...] = dot(z_t[...], ca[...]).reshape(2, 2, 2, 16, D)
    os1[...] = go[:, :, 1 - k].astype(BF16)
    go_k = send(os1, or1, core)

    for kt in range(4):
        def back_step(qt, carry, kt=kt):
            attend_back(a, kt, qt, BASE[kt] + qt - kt, dkv_own)
            return carry

        lax.fori_loop(kt, 4, back_step, 0)

    arrive([go_k])
    go[:, :, k] = go[:, :, k] + or1[...].astype(F32)
    for there in range(4):
        os2[there] = go[:, there % 2, k, :, (there // 2) * 256 : (there // 2 + 1) * 256].astype(BF16)
    go_x = [send(os2.at[(x + s) % 4], or2.at[s - 1], at_x(s)) for s in (1, 2, 3)]

    for i in range(4):
        rows = pl.ds(i * 256, 256)
        dpre[rows, 128:256] = ((dq_t[:, rows] * SCALE).T * slope[rows, 0:128]).astype(BF16)

    def grad_start(grads, first_column, n):
        for i in range(2):
            rows = pl.ds(i * 256, 256)
            part = dot(xt[rows, :], dpre[:, first_column : first_column + 256])
            grads[i * 4 : (i + 1) * 4] = part.reshape(4, 2, 2, 16, 256)
        s1[n] = grads[:, :, 1 - k].astype(BF16)
        return send(s1.at[n], r1.at[n], core)

    def grad_x(grads, n, copy):
        arrive([copy])
        grads[:, :, k] = grads[:, :, k] + r1[n].astype(F32)
        for there in range(4):
            s2[n, there] = grads[
                :, there % 2, k, :, (there // 2) * 128 : (there // 2 + 1) * 128
            ].astype(BF16)
        return [send(s2.at[n, (x + s) % 4], r2.at[n, s - 1], at_x(s)) for s in (1, 2, 3)]

    def grad_z(grads, n, copies):
        arrive(copies)
        total = grads[:, xl, k, :, pl.ds(pl.multiple_of(a * 128, 128), 128)]
        total = total + r2[n, 0].astype(F32) + r2[n, 1].astype(F32) + r2[n, 2].astype(F32)
        tot[n] = total
        s3[n] = total.astype(BF16)
        return [send(s3.at[n, (z + s) % NZ], r3.at[n, s - 1], at_z(s)) for s in range(1, NZ)]

    def grad_ctx(n, copies):
        arrive(copies)
        total = tot[n, z]
        for s in range(NZ - 1):
            total = total + r3[n, s].astype(F32)
        fr[n, cx] = total
        return [send(fr.at[n, cx], fr.at[n, cx], at_ctx(s)) for s in range(1, 8)]

    def grad_end(n, copies):
        arrive(copies)
        for c in range(8):
            first = (n * 2 + c // 4) * D + (c % 4) * 128
            gi_out[:, first : first + 128] = fr[n, c]

    ga_k = grad_start(ga, 0, 0)

    arrive(go_x)
    total = go[:, xl, k, :, pl.ds(pl.multiple_of(a * 256, 256), 256)]
    total = total + or2[0].astype(F32) + or2[1].astype(F32) + or2[2].astype(F32)
    otot[...] = total
    os3[...] = total.astype(BF16)
    go_first = sems(NZ)
    go_sent = sems(2)

    def go_copy(j):
        return remote(os3.at[j], or3.at[z], at_zabs(2 * y + j), go_sent + j, go_first + z)

    for j in range(2):
        @pl.when(z != 2 * y + j)
        def _():
            go_copy(j).start()

    ga_x = grad_x(ga, 0, ga_k)
    go_end_first = sems(8)
    go_end_recv = sems(2)

    def go_end(s):
        return remote(ofr.at[a], ofr.at[a], at_ctx(s), go_end_first + s, go_end_recv + a)

    @pl.when(owner)
    def _():
        final = otot[z % 2]
        for s in range(1, NZ):
            source = (z + s) % NZ
            remote(
                os3.at[0], or3.at[source], at_z(s), go_sent, go_first + source
            ).wait_recv()
            final = final + or3[source].astype(F32)
        ofr[a] = final
        for s in range(1, 8):
            go_end(s).start()

    ga_z = grad_z(ga, 0, ga_x)

    for i in range(4):
        rows = pl.ds(i * 256, 256)
        arrive([dkv_x[i]])
        both = dkv_own[rows, :] + dkv_r[rows, :].astype(F32)
        dpre[rows, 256:384] = (both[:, 0:128] * SCALE * slope[rows, 128:256]).astype(BF16)
        dpre[rows, 384:512] = (both[:, 128:256] * slope[rows, 256:384]).astype(BF16)
        part = dot(dpre[rows, :], w5[...].reshape(D, D), NT)
        dx_f[rows, :] = part
        dx_s[rows, :] = part.astype(BF16)
    dx_y = []
    for s in (1, 3, 2):
        to_early, to_late = slots(s)
        dx_y.append(send(dx_s.at[to_early], dx_r.at[s - 1, pl.ds(0, 128)], at_y(s)))
        dx_y.append(send(dx_s.at[to_late], dx_r.at[s - 1, pl.ds(128, 128)], at_y(s)))
    gb_k = grad_start(gb, 256, 1)
    ga_c = grad_ctx(0, ga_z)
    gb_x = grad_x(gb, 1, gb_k)

    arrive(lo_y)
    for i, rows in enumerate((early, late)):
        own = pl.ds(i * 128, 128)
        total = lo_f[rows, :] + tok[own, :].astype(F32)
        for j in range(3):
            total = total + lo_r[j, own, :].astype(F32)
        lo_out[own, :] = total.astype(BF16)

    gb_z = grad_z(gb, 1, gb_x)
    grad_end(0, ga_c)
    for other in range(2):
        @pl.when(jnp.logical_or(z // 2 != y, a != other))
        def _():
            remote(
                ofr.at[other], ofr.at[other], at_ctx(1), go_end_first, go_end_recv + other
            ).wait_recv()

        go_out[:, other * 256 : (other + 1) * 256] = ofr[other]
    gb_c = grad_ctx(1, gb_z)

    arrive(dx_y)
    for i, rows in enumerate((early, late)):
        own = pl.ds(i * 128, 128)
        total = dx_f[rows, :]
        for j in range(3):
            total = total + dx_r[j, own, :].astype(F32)
        xn, r = normed(own)
        first_mean = jnp.mean(total, axis=-1, keepdims=True)
        second_mean = jnp.mean(total * xn, axis=-1, keepdims=True)
        total = r * (total - first_mean - xn * second_mean) + cot[own, :].astype(F32)
        dt_out[own, :] = total.astype(BF16)
    grad_end(1, gb_c)

    for copy in started:
        copy.wait_send()

    @pl.when(owner)
    def _():
        for s in range(1, NZ):
            wo_copy(s).wait_send()
        for s in range(1, 8):
            go_end(s).wait_send()

    for j in range(2):
        @pl.when(z != 2 * y + j)
        def _():
            go_copy(j).wait_send()


N_SEMS = 136
SCRATCH = dict(
    xa=((1024, D), BF16), ca=((1024, D), BF16), xt=((D, 1024), BF16),
    w5=((NZ, 2, 2, 16, D), BF16), wo5=((2, 2, 2, 16, D), BF16), wgt=((128, D), BF16),
    kv=((2, 1024, 256), BF16), kvt=((2, 256, 1024), BF16), qs=((1024, 128), BF16),
    slope=((1024, 384), F32), gate_t=((128, 1024), F32), slope_gt=((128, 1024), F32),
    dg_t=((128, 1024), F32), dz_t=((128, 1024), F32),
    at=((18, 256, 256), BF16), sl=((18, 256, 256), F32), mixed_t=((128, 1024), F32),
    stats=((4, 8, 1024), F32), dm_t=((128, 1024), BF16), z_t=((128, 1024), BF16),
    dq_t=((128, 1024), F32), dkv_own=((1024, 256), F32), dkv_far=((1024, 256), F32),
    dkv_s=((1024, 256), BF16), dkv_r=((1024, 256), BF16),
    lo_f=((1024, D), F32), lo_s=((1024, D), BF16), lo_r=((3, 256, D), BF16),
    dpre=((1024, D), BF16), dx_f=((1024, D), F32), dx_s=((1024, D), BF16), dx_r=((3, 256, D), BF16),
    ga=((NZ, 2, 2, 16, 256), F32), gb=((NZ, 2, 2, 16, 256), F32),
    s1=((2, NZ, 2, 16, 256), BF16), r1=((2, NZ, 2, 16, 256), BF16),
    s2=((2, 4, NZ, 16, 128), BF16), r2=((2, 3, NZ, 16, 128), BF16), tot=((2, NZ, 16, 128), F32),
    s3=((2, NZ, 16, 128), BF16), r3=((2, NZ - 1, 16, 128), BF16), fr=((2, 8, 16, 128), F32),
    go=((2, 2, 2, 16, D), F32), os1=((2, 2, 16, D), BF16), or1=((2, 2, 16, D), BF16),
    os2=((4, 2, 16, 256), BF16), or2=((3, 2, 16, 256), BF16), otot=((2, 16, 256), F32),
    os3=((2, 16, 256), BF16), or3=((NZ, 16, 256), BF16), ofr=((2, 16, 256), F32),
)


def body(tokens, seq_lengths, w_in, w_out, cotangent):
    vmem = pl.BlockSpec(memory_space=pltpu.VMEM)
    return pl.pallas_call(
        kernel,
        name="hstu",
        out_shape=(
            jax.ShapeDtypeStruct((256, D), BF16),
            jax.ShapeDtypeStruct((256, D), BF16),
            jax.ShapeDtypeStruct((16, 4 * D), F32),
            jax.ShapeDtypeStruct((16, D), F32),
        ),
        in_specs=[vmem, pl.BlockSpec(memory_space=pltpu.SMEM), vmem, vmem, vmem],
        out_specs=(vmem, vmem, vmem, vmem),
        scratch_shapes=[pltpu.VMEM(*spec) for spec in SCRATCH.values()]
        + [pltpu.SemaphoreType.DMA((N_SEMS,)), pltpu.SemaphoreType.DMA((N_SEMS,))],
        compiler_params=pltpu.CompilerParams(
            collective_id=0, has_side_effects=True, vmem_limit_bytes=56 * 2**20
        ),
    )(tokens, seq_lengths, w_in, w_out, cotangent)


def solution(mesh):
    return jax.shard_map(
        body,
        mesh=mesh,
        in_specs=(
            P(("dp", "ctx"), None),
            P("dp", None),
            P("dp", None),
            P("dp", None),
            P(("dp", "ctx"), None),
        ),
        out_specs=(P(("dp", "ctx"), None), P(("dp", "ctx"), None), P("dp", None), P("dp", None)),
        check_vma=False,
    )
```

```python
import math

import jax
import jax.numpy as jnp
from jax import lax
from jax.experimental import pallas as pl
from jax.experimental.pallas import tpu as pltpu
from jax.sharding import PartitionSpec as P

MESH = pl.DeviceIdType.MESH
F32 = jnp.float32
BF16 = jnp.bfloat16
EPS = 1e-05
NZ = 8
D = 512
H = 128
SCALE = 1.0 / math.sqrt(H)
NN = (((1,), (0,)), ((), ()))
NT = (((1,), (1,)), ((), ()))
BASE = (0, 4, 7, 9)


def dot(lhs, rhs, dims=NN):
    return lax.dot_general(lhs, rhs, dims, preferred_element_type=F32)


def sigmoid(v):
    return 0.5 * jnp.tanh(0.5 * v) + 0.5


def kernel(
    tok, seq, win, wout, cot, lo_hbm, dt_hbm, gi_hbm, go_hbm,
    xa, ca, xt, w5, wo5, wgt, kv, kvt, qs, slope, gate_t, slope_gt, dg_t, dz_t,
    at, sl, at_far, sl_far, mixed_t, stats, dm_t, z_t, z_r, g_r, dq_t, dkv_own, dkv_far, dkv_s, dkv_r,
    dpre, dx_f, dx_s, dx_r,
    ga, gb, s1, r1, s2, r2, tot, s3, r3, fr,
    go, os1, or1, os2, or2, otot, os3, or3, ofr,
    lo_out, dt_out, gi_out, go_out,
    ssem, rsem, osem,
):
    dp = lax.axis_index("dp")
    cx = lax.axis_index("ctx")
    z, xl, k = dp // 4, (dp // 2) % 2, dp % 2
    a, y = cx // 4, cx % 4
    x = a * 2 + xl

    def at_y(s):
        return {"dp": dp, "ctx": a * 4 + (y + s) % 4}

    def at_x(s):
        there = (x + s) % 4
        return {"dp": z * 4 + (there % 2) * 2 + k, "ctx": (there // 2) * 4 + y}

    def at_z(s):
        return {"dp": ((z + s) % NZ) * 4 + xl * 2 + k, "ctx": cx}

    def at_zabs(there):
        return {"dp": there * 4 + xl * 2 + k, "ctx": cx}

    def at_ctx(s):
        return {"dp": dp, "ctx": (cx + s) % 8}

    core = {"dp": z * 4 + xl * 2 + (1 - k), "ctx": cx}
    xl_mate = {"dp": z * 4 + (1 - xl) * 2 + k, "ctx": cx}
    diagonal_mate = {"dp": z * 4 + (1 - xl) * 2 + (1 - k), "ctx": cx}
    far = {"dp": dp, "ctx": (1 - a) * 4 + y}

    peers = [core, diagonal_mate, at_x(1), at_x(3)]
    peers += [at_z(s) for s in range(1, NZ)]
    peers += [at_ctx(s) for s in range(1, 8)]
    barrier = pltpu.get_barrier_semaphore()
    for peer in peers:
        pl.semaphore_signal(barrier, inc=1, device_id=peer, device_id_type=MESH)

    counter = [0]
    started = []

    def sems(n=1):
        first = counter[0]
        counter[0] += n
        return first

    def remote(src, dst, peer, s_index, r_index):
        return pltpu.make_async_remote_copy(
            src_ref=src, dst_ref=dst, send_sem=ssem.at[s_index], recv_sem=rsem.at[r_index],
            device_id=peer, device_id_type=MESH,
        )

    def send(src, dst, peer):
        i = sems()
        copy = remote(src, dst, peer, i, i)
        copy.start()
        started.append(copy)
        return copy

    def arrive(copies):
        for copy in copies:
            copy.wait_recv()

    early = pl.ds(pl.multiple_of(y * 128, 128), 128)
    late = pl.ds(pl.multiple_of((7 - y) * 128, 128), 128)

    def slots(s):
        there = (y + s) % 4
        return (
            pl.ds(pl.multiple_of(there * 128, 128), 128),
            pl.ds(pl.multiple_of((7 - there) * 128, 128), 128),
        )

    for part, block in enumerate((2, 3, 0, 1)):
        w5[z, xl, k, :, part * 128 : (part + 1) * 128] = win[
            :, pl.ds(pl.multiple_of(block * D + y * 128, 128), 128)
        ]
    wo5[z, xl, k] = wout[...]
    owner = z // 2 == y

    def normed(rows):
        v = tok[rows, :].astype(F32)
        centre = v - jnp.mean(v, axis=-1, keepdims=True)
        spread = lax.rsqrt(jnp.mean(centre * centre, axis=-1, keepdims=True) + EPS)
        return centre * spread, spread

    xa[early, :] = normed(pl.ds(0, 128))[0].astype(BF16)
    xa[late, :] = normed(pl.ds(128, 128))[0].astype(BF16)
    ca[early, :] = cot[0:128, :]
    ca[late, :] = cot[128:256, :]

    pl.semaphore_wait(barrier, len(peers))

    front, back = pl.ds(0, 256), pl.ds(256, 256)

    z_order = (4, 3, 5, 2, 6, 1, 7)

    def along_z(ref, *columns):
        part = ref.at[z, xl, k, :, *columns]
        return [send(part, part, at_z(s)) for s in z_order]

    def along_x(ref, *columns):
        part = ref.at[:, xl, k, :, *columns]
        return send(part, part, xl_mate)

    def to_core(ref, *columns):
        part = ref.at[:, :, k, :, *columns]
        return send(part, part, core)

    def onward(there):
        part = w5.at[there, xl, k, :, front]
        return [send(part, part, mate) for mate in (xl_mate, diagonal_mate, core)]

    order = (0, 1, 3, 2)
    kv_z = along_z(w5, front)
    kv_w = onward(z)
    x_y = {}
    for s in order[1:]:
        x_y[s] = [send(xa.at[early], xa.at[early], at_y(s)), send(xa.at[late], xa.at[late], at_y(s))]
    gq_z = along_z(w5, back)
    for s in (1, 7, 2, 6, 3, 5, 4):
        arrive([kv_z[z_order.index(s)]])
        kv_w += onward((z - s) % NZ)
    wo_z = along_z(wo5)
    arrive(gq_z)
    gq_w = along_x(w5, back)
    arrive(kv_w)

    def place_of(s):
        return (y - s) % 4

    def rows_of(block):
        return (
            pl.ds(pl.multiple_of(block * 128, 128), 128),
            pl.ds(pl.multiple_of((7 - block) * 128, 128), 128),
        )

    def kv_late(rows, index):
        return remote(kv.at[a, rows], kv.at[a, rows], far, index, index)

    late_first = sems(4)
    kv_x = []
    w_kv = w5[:, :, :, :, 0:256].reshape(D, 256)
    for i, s in enumerate(order):
        if s:
            arrive(x_y[s])
        if i == 3:
            c_y = []
            for t in order[1:]:
                c_y.append(send(ca.at[early], ca.at[early], at_y(t)))
                c_y.append(send(ca.at[late], ca.at[late], at_y(t)))
        first, last = rows_of(place_of(s))
        for rows in (first, last):
            pre = dot(xa[rows, :], w_kv)
            sig = sigmoid(pre)
            act = pre * sig
            kv[a, rows, :] = act.astype(BF16)
            slope[rows, 128:384] = sig + act * (1.0 - sig)
        kv_x.append(send(kv.at[a, first], kv.at[a, first], far))

        @pl.when(a == 1)
        def _():
            kv_late(last, late_first + i).start()

    arrive([gq_w])
    gq_w = to_core(w5, back)
    arrive(wo_z)
    wo_w = along_x(wo5)
    arrive([gq_w])
    wgt[...] = w5[:, :, :, :, 256:384].reshape(D, 128).T
    for i in range(4):
        rows = pl.ds(i * 256, 256)
        pre = dot(xa[rows, :], w5[:, :, :, :, 384:512].reshape(D, 128))
        sig = sigmoid(pre)
        act = pre * sig
        qs[rows, :] = act.astype(BF16)
        slope[rows, 0:128] = sig + act * (1.0 - sig)
        pre = dot(wgt[...], xa[rows, :], NT)
        sig = sigmoid(pre)
        act = pre * sig
        gate_t[:, rows] = act.astype(BF16).astype(F32)
        slope_gt[:, rows] = sig + act * (1.0 - sig)
        kvt[a, :, rows] = kv[a, rows, :].T
        xt[:, rows] = xa[rows, :].T
    arrive([wo_w])
    wo_w = to_core(wo5)

    mixed_t[...] = jnp.zeros_like(mixed_t)
    border = seq[0, 0]

    def tile(i):
        return pl.ds(pl.multiple_of(i * 256, 256), 256)

    def place(half, i):
        return i * 256 + half * 512 + (1 - half) * 1024 * (i // 2)

    def attend(half, kt, qt, index, diagonal):
        scores = dot(kv[half, tile(kt), 0:128], qs[tile(qt), :], NT)
        key_at = lax.broadcasted_iota(jnp.int32, (256, 256), 0) + place(half, kt)
        query_at = lax.broadcasted_iota(jnp.int32, (1, 256), 1) + place(a, qt)
        least = jnp.where(query_at >= border, border, 0)
        allowed = key_at >= least
        if diagonal:
            allowed = allowed & (key_at <= query_at)
        s = scores * SCALE
        sig = jnp.where(allowed, sigmoid(s), 0.0)
        act = s * sig
        act_b = act.astype(BF16)
        at[index] = act_b
        sl[index] = sig + act * (1.0 - sig)
        mixed_t[:, tile(qt)] += dot(kvt[half, 128:256, tile(kt)], act_b)

    for kt in range(4):
        for qt in range(kt, 4):
            attend(a, kt, qt, BASE[kt] + qt - kt, qt == kt)

    def far_tile(block, j):
        key_slot = block + (1 - a) * j * (7 - 2 * block)
        query_first = (1 - a + a * j) * 512
        return (
            key_slot,
            pl.ds(pl.multiple_of(key_slot * 128, 128), 128),
            pl.ds(pl.multiple_of(query_first, 512), 512),
            query_first,
        )

    def slot_place(half, slot):
        return slot * 128 + half * 512 + (1 - half) * 1024 * (slot // 4)

    for i, s in enumerate(order):
        block = place_of(s)
        first, last = rows_of(block)
        arrive([kv_x[i]])
        kvt[1 - a, :, first] = kv[1 - a, first, :].T

        @pl.when(a == 0)
        def _():
            kv_late(last, late_first + i).wait_recv()
            kvt[1, :, last] = kv[1, last, :].T

        for j in range(2):
            slot, keys, queries, query_first = far_tile(block, j)
            s_t = dot(kv[1 - a, keys, 0:128], qs[queries, :], NT) * SCALE
            key_at = lax.broadcasted_iota(jnp.int32, (128, 512), 0) + slot_place(1 - a, slot)
            query_at = lax.broadcasted_iota(jnp.int32, (1, 512), 1) + slot_place(a, query_first // 128)
            sig = jnp.where(key_at >= jnp.where(query_at >= border, border, 0), sigmoid(s_t), 0.0)
            act = s_t * sig
            act_b = act.astype(BF16)
            at_far[2 * i + j] = act_b
            sl_far[2 * i + j] = sig + act * (1.0 - sig)
            mixed_t[:, queries] += dot(kvt[1 - a, 128:256, keys], act_b)

    arrive(c_y)
    arrive([wo_w])
    head = pl.ds(pl.multiple_of(y * 2, 2), 2)
    for i in range(4):
        rows = pl.ds(i * 256, 256)
        part = dot(wo5[head].reshape(128, D), ca[rows, :], NT)
        dg_t[:, rows] = part
        dz_t[:, rows] = part * gate_t[:, rows]
    mixed = mixed_t[...]
    mean_h = jnp.mean(mixed, axis=0, keepdims=True)
    centred = mixed - mean_h
    dz = dz_t[...]
    stats[y, 0:1, :] = mean_h
    stats[y, 1:2, :] = jnp.sum(centred * centred, axis=0, keepdims=True)
    stats[y, 2:3, :] = jnp.sum(dz, axis=0, keepdims=True)
    stats[y, 3:4, :] = jnp.sum(dz * centred, axis=0, keepdims=True)
    stats[y, 4:8, :] = jnp.zeros((4, 1024), F32)
    arrive([send(stats.at[y], stats.at[y], at_y(s)) for s in (1, 2, 3)])
    means = [stats[j, 0:1, :] for j in range(4)]
    mean = (means[0] + means[1] + means[2] + means[3]) * 0.25
    second = jnp.zeros((1, 1024), F32)
    first_dz = jnp.zeros((1, 1024), F32)
    second_dz = jnp.zeros((1, 1024), F32)
    for j in range(4):
        off = means[j] - mean
        second += stats[j, 1:2, :] + 128.0 * off * off
        first_dz += stats[j, 2:3, :]
        second_dz += stats[j, 3:4, :] + off * stats[j, 2:3, :]
    spread = lax.rsqrt(second * (1.0 / D) + EPS)
    first_dz = first_dz * (1.0 / D)
    second_dz = second_dz * (1.0 / D) * spread
    for i in range(4):
        rows = pl.ds(i * 256, 256)
        r = spread[:, i * 256 : (i + 1) * 256]
        zn = (mixed_t[:, rows] - mean[:, i * 256 : (i + 1) * 256]) * r
        z_t[:, rows] = (zn * gate_t[:, rows]).astype(BF16)
        dm_t[:, rows] = (
            r * (
                dz_t[:, rows] - first_dz[:, i * 256 : (i + 1) * 256]
                - zn * second_dz[:, i * 256 : (i + 1) * 256]
            )
        ).astype(BF16)
        dpre[rows, 256:384] = (dg_t[:, rows] * zn * slope_gt[:, rows]).astype(BF16).T

    dq_t[...] = jnp.zeros_like(dq_t)
    dkv_own[...] = jnp.zeros_like(dkv_own)
    dkv_far[...] = jnp.zeros_like(dkv_far)

    def attend_back(half, kt, qt, index, grads):
        d_attn = dot(kv[half, tile(kt), 128:256], dm_t[:, tile(qt)])
        ds = (d_attn * sl[index]).astype(BF16)
        grads[tile(kt), 128:256] += dot(at[index], dm_t[:, tile(qt)], NT)
        grads[tile(kt), 0:128] += dot(ds, qs[tile(qt), :])
        dq_t[:, tile(qt)] += dot(kvt[half, 0:128, tile(kt)], ds)

    def dkv_late(rows, index):
        return remote(dkv_s.at[rows], dkv_r.at[rows], far, index, index)

    @pl.when(a == 0)
    def _():
        dkv_r[512:1024, :] = jnp.zeros((512, 256), BF16)

    back_order = (2, 1, 3, 0)
    dkv_late_first = sems(4)
    dkv_x = []
    for i, s in enumerate(back_order):
        block = (y + s) % 4
        first, last = rows_of(block)
        index = 2 * order.index((4 - s) % 4)
        for j in range(2):
            slot, keys, queries, _ = far_tile(block, j)
            d_attn = dot(kv[1 - a, keys, 128:256], dm_t[:, queries])
            ds = (d_attn * sl_far[index + j]).astype(BF16)
            dkv_far[keys, 128:256] += dot(at_far[index + j], dm_t[:, queries], NT)
            dkv_far[keys, 0:128] += dot(ds, qs[queries, :])
            dq_t[:, queries] += dot(kvt[1 - a, 0:128, keys], ds)
        dkv_s[first, :] = dkv_far[first, :].astype(BF16)
        dkv_x.append(send(dkv_s.at[first], dkv_r.at[first], far))

        @pl.when(a == 0)
        def _():
            dkv_s[last, :] = dkv_far[last, :].astype(BF16)
            dkv_late(last, dkv_late_first + i).start()

    z_r[...] = z_t[...].T
    g_r[y, 0:128, :] = z_r[early, :]
    g_r[y, 128:256, :] = z_r[late, :]
    g_y = []
    for s in order[1:]:
        to_early, to_late = slots(s)
        g_y.append(send(z_r.at[to_early], g_r.at[y, pl.ds(0, 128)], at_y(s)))
        g_y.append(send(z_r.at[to_late], g_r.at[y, pl.ds(128, 128)], at_y(s)))
    for kt in range(4):
        for qt in range(kt, 4):
            attend_back(a, kt, qt, BASE[kt] + qt - kt, dkv_own)

    for i in range(4):
        rows = pl.ds(i * 256, 256)
        dpre[rows, 384:512] = ((dq_t[:, rows] * SCALE).T * slope[rows, 0:128]).astype(BF16)

    def grad_start(grads, first_column, n):
        for i in range(2):
            rows = pl.ds(i * 256, 256)
            part = dot(xt[rows, :], dpre[:, first_column : first_column + 256])
            grads[i * 4 : (i + 1) * 4] = part.reshape(4, 2, 2, 16, 256)
        s1[n] = grads[:, :, 1 - k].astype(BF16)
        return send(s1.at[n], r1.at[n], core)

    def grad_x(grads, n, copy):
        arrive([copy])
        grads[:, :, k] = grads[:, :, k] + r1[n].astype(F32)
        for there in range(4):
            s2[n, there] = grads[
                :, there % 2, k, :, (there // 2) * 128 : (there // 2 + 1) * 128
            ].astype(BF16)
        return [send(s2.at[n, (x + s) % 4], r2.at[n, s - 1], at_x(s)) for s in (1, 2, 3)]

    def grad_z(grads, n, copies):
        arrive(copies)
        total = grads[:, xl, k, :, pl.ds(pl.multiple_of(a * 128, 128), 128)]
        total = total + r2[n, 0].astype(F32) + r2[n, 1].astype(F32) + r2[n, 2].astype(F32)
        tot[n] = total
        s3[n] = total.astype(BF16)
        return [send(s3.at[n, (z + s) % NZ], r3.at[n, s - 1], at_z(s)) for s in range(1, NZ)]

    def grad_ctx(n, copies):
        arrive(copies)
        total = tot[n, z]
        for s in range(NZ - 1):
            total = total + r3[n, s].astype(F32)
        fr[n, cx] = total
        return [send(fr.at[n, cx], fr.at[n, cx], at_ctx(s)) for s in range(1, 8)]

    def grad_end(n, copies):
        arrive(copies)
        for c in range(8):
            first = (n * 2 + c // 4) * D + (c % 4) * 128
            gi_out[:, first : first + 128] = fr[n, c]

    go_end_first = sems(8)
    go_end_recv = sems(2)

    def go_end(s):
        return remote(ofr.at[a], ofr.at[a], at_ctx(s), go_end_first + s, go_end_recv + a)


    dx_y = []
    w_t = w5[...].reshape(D, D)
    for i, s in enumerate(back_order):
        first, last = rows_of((y + s) % 4)
        arrive([dkv_x[i]])

        @pl.when(a == 1)
        def _():
            dkv_late(last, dkv_late_first + i).wait_recv()

        for half, rows in enumerate((first, last)):
            both = dkv_own[rows, :] + dkv_r[rows, :].astype(F32)
            dpre[rows, 0:128] = (both[:, 0:128] * SCALE * slope[rows, 128:256]).astype(BF16)
            dpre[rows, 128:256] = (both[:, 128:256] * slope[rows, 256:384]).astype(BF16)
            if s:
                dx_s[rows, :] = dot(dpre[rows, :], w_t, NT).astype(BF16)
                own = pl.ds(half * 128, 128)
                dx_y.append(send(dx_s.at[rows], dx_r.at[s - 1, own], at_y(s)))
        if i == 1:
            go[...] = dot(z_t[...], ca[...]).reshape(2, 2, 2, 16, D)
            os1[...] = go[:, :, 1 - k].astype(BF16)
            go_k = send(os1, or1, core)
        if i == 2:
            ga_k = grad_start(ga, 256, 0)
    gb_k = grad_start(gb, 0, 1)
    for half, rows in enumerate((early, late)):
        dx_f[half * 128 : (half + 1) * 128, :] = dot(dpre[rows, :], w_t, NT)
    arrive([go_k])
    go[:, :, k] = go[:, :, k] + or1[...].astype(F32)
    for there in range(4):
        os2[there] = go[:, there % 2, k, :, (there // 2) * 256 : (there // 2 + 1) * 256].astype(BF16)
    go_x = [send(os2.at[(x + s) % 4], or2.at[s - 1], at_x(s)) for s in (1, 2, 3)]
    ga_x = grad_x(ga, 0, ga_k)
    gb_x = grad_x(gb, 1, gb_k)
    arrive(go_x)
    total = go[:, xl, k, :, pl.ds(pl.multiple_of(a * 256, 256), 256)]
    total = total + or2[0].astype(F32) + or2[1].astype(F32) + or2[2].astype(F32)
    otot[...] = total
    os3[...] = total.astype(BF16)
    go_first = sems(NZ)
    go_sent = sems(2)

    def go_copy(j):
        return remote(os3.at[j], or3.at[z], at_zabs(2 * y + j), go_sent + j, go_first + z)

    for j in range(2):
        @pl.when(z != 2 * y + j)
        def _():
            go_copy(j).start()

    arrive(g_y)
    for own in (pl.ds(0, 128), pl.ds(128, 128)):
        total = tok[own, :].astype(F32)
        for h in range(4):
            total = total + dot(g_r[h, own, :], wo5[2 * h : 2 * h + 2].reshape(128, D))
        lo_out[own, :] = total.astype(BF16)
    to_hbm = [pltpu.make_async_copy(lo_out, lo_hbm, osem.at[0])]
    to_hbm[0].start()
    ga_z = grad_z(ga, 0, ga_x)
    gb_z = grad_z(gb, 1, gb_x)
    @pl.when(owner)
    def _():
        final = otot[z % 2]
        for s in range(1, NZ):
            source = (z + s) % NZ
            remote(
                os3.at[0], or3.at[source], at_z(s), go_sent, go_first + source
            ).wait_recv()
            final = final + or3[source].astype(F32)
        ofr[a] = final
        for s in range(1, 8):
            go_end(s).start()

    ga_c = grad_ctx(0, ga_z)
    arrive(dx_y)
    for i, rows in enumerate((early, late)):
        own = pl.ds(i * 128, 128)
        total = dx_f[own, :]
        for j in range(3):
            total = total + dx_r[j, own, :].astype(F32)
        xn, r = normed(own)
        first_mean = jnp.mean(total, axis=-1, keepdims=True)
        second_mean = jnp.mean(total * xn, axis=-1, keepdims=True)
        total = r * (total - first_mean - xn * second_mean) + cot[own, :].astype(F32)
        dt_out[own, :] = total.astype(BF16)
    to_hbm.append(pltpu.make_async_copy(dt_out, dt_hbm, osem.at[2]))
    to_hbm[-1].start()
    gb_c = grad_ctx(1, gb_z)
    for other in range(2):
        @pl.when(jnp.logical_or(z // 2 != y, a != other))
        def _():
            remote(
                ofr.at[other], ofr.at[other], at_ctx(1), go_end_first, go_end_recv + other
            ).wait_recv()

        go_out[:, other * 256 : (other + 1) * 256] = ofr[other]
    to_hbm.append(pltpu.make_async_copy(go_out, go_hbm, osem.at[1]))
    to_hbm[-1].start()
    grad_end(0, ga_c)
    grad_end(1, gb_c)
    to_hbm.append(pltpu.make_async_copy(gi_out, gi_hbm, osem.at[3]))
    to_hbm[-1].start()

    for copy in started:
        copy.wait_send()

    @pl.when(a == 1)
    def _():
        for i, s in enumerate(order):
            kv_late(rows_of(place_of(s))[1], late_first + i).wait_send()

    @pl.when(a == 0)
    def _():
        for i, s in enumerate(back_order):
            dkv_late(rows_of((y + s) % 4)[1], dkv_late_first + i).wait_send()

    @pl.when(owner)
    def _():
        for s in range(1, 8):
            go_end(s).wait_send()

    for j in range(2):
        @pl.when(z != 2 * y + j)
        def _():
            go_copy(j).wait_send()

    for copy in to_hbm:
        copy.wait()


N_SEMS = 200
SCRATCH = dict(
    xa=((1024, D), BF16), ca=((1024, D), BF16), xt=((D, 1024), BF16),
    w5=((NZ, 2, 2, 16, D), BF16), wo5=((NZ, 2, 2, 16, D), BF16), wgt=((128, D), BF16),
    kv=((2, 1024, 256), BF16), kvt=((2, 256, 1024), BF16), qs=((1024, 128), BF16),
    slope=((1024, 384), F32), gate_t=((128, 1024), F32), slope_gt=((128, 1024), F32),
    dg_t=((128, 1024), F32), dz_t=((128, 1024), F32),
    at=((10, 256, 256), BF16), sl=((10, 256, 256), F32),
    at_far=((8, 128, 512), BF16), sl_far=((8, 128, 512), F32), mixed_t=((128, 1024), F32),
    stats=((4, 8, 1024), F32), dm_t=((128, 1024), BF16), z_t=((128, 1024), BF16),
    z_r=((1024, 128), BF16), g_r=((4, 256, 128), BF16),
    dq_t=((128, 1024), F32), dkv_own=((1024, 256), F32), dkv_far=((1024, 256), F32),
    dkv_s=((1024, 256), BF16), dkv_r=((1024, 256), BF16),
    dpre=((1024, D), BF16), dx_f=((256, D), F32), dx_s=((1024, D), BF16), dx_r=((3, 256, D), BF16),
    ga=((NZ, 2, 2, 16, 256), F32), gb=((NZ, 2, 2, 16, 256), F32),
    s1=((2, NZ, 2, 16, 256), BF16), r1=((2, NZ, 2, 16, 256), BF16),
    s2=((2, 4, NZ, 16, 128), BF16), r2=((2, 3, NZ, 16, 128), BF16), tot=((2, NZ, 16, 128), F32),
    s3=((2, NZ, 16, 128), BF16), r3=((2, NZ - 1, 16, 128), BF16), fr=((2, 8, 16, 128), F32),
    go=((2, 2, 2, 16, D), F32), os1=((2, 2, 16, D), BF16), or1=((2, 2, 16, D), BF16),
    os2=((4, 2, 16, 256), BF16), or2=((3, 2, 16, 256), BF16), otot=((2, 16, 256), F32),
    os3=((2, 16, 256), BF16), or3=((NZ, 16, 256), BF16), ofr=((2, 16, 256), F32),
    lo_out=((256, D), BF16), dt_out=((256, D), BF16), gi_out=((16, 4 * D), F32), go_out=((16, D), F32),
)


def move(*refs):
    for source, target in zip(refs[:4], refs[4:]):
        target[...] = source[...]


def body(tokens, seq_lengths, w_in, w_out, cotangent):
    vmem = pl.BlockSpec(memory_space=pltpu.VMEM)
    anywhere = pl.BlockSpec(memory_space=pl.ANY)
    outs = (
        jax.ShapeDtypeStruct((256, D), BF16),
        jax.ShapeDtypeStruct((256, D), BF16),
        jax.ShapeDtypeStruct((16, 4 * D), F32),
        jax.ShapeDtypeStruct((16, D), F32),
    )
    results = pl.pallas_call(
        kernel,
        name="hstu",
        out_shape=outs,
        in_specs=[vmem, pl.BlockSpec(memory_space=pltpu.SMEM), vmem, vmem, vmem],
        out_specs=(anywhere,) * 4,
        scratch_shapes=[pltpu.VMEM(*spec) for spec in SCRATCH.values()]
        + [pltpu.SemaphoreType.DMA((n,)) for n in (N_SEMS, N_SEMS, 4)],
        compiler_params=pltpu.CompilerParams(
            collective_id=0, has_side_effects=True, vmem_limit_bytes=56 * 2**20
        ),
    )(tokens, seq_lengths, w_in, w_out, cotangent)
    return pl.pallas_call(
        move,
        name="move",
        out_shape=outs,
        in_specs=[vmem] * 4,
        out_specs=(vmem,) * 4,
    )(*results)


def solution(mesh):
    return jax.shard_map(
        body,
        mesh=mesh,
        in_specs=(
            P(("dp", "ctx"), None),
            P("dp", None),
            P("dp", None),
            P("dp", None),
            P(("dp", "ctx"), None),
        ),
        out_specs=(P(("dp", "ctx"), None), P(("dp", "ctx"), None), P("dp", None), P("dp", None)),
        check_vma=False,
    )
```

```python
import math

import jax
import jax.numpy as jnp
from jax import lax
from jax.experimental import pallas as pl
from jax.experimental.pallas import tpu as pltpu
from jax.sharding import PartitionSpec as P

MESH = pl.DeviceIdType.MESH
F32 = jnp.float32
BF16 = jnp.bfloat16
EPS = 1e-05
NZ = 8
D = 512
H = 128
SCALE = 1.0 / math.sqrt(H)
NN = (((1,), (0,)), ((), ()))
NT = (((1,), (1,)), ((), ()))
BASE = (0, 4, 7, 9)


def dot(lhs, rhs, dims=NN):
    return lax.dot_general(lhs, rhs, dims, preferred_element_type=F32)


def sigmoid(v):
    return 0.5 * jnp.tanh(0.5 * v) + 0.5


def kernel(
    tok, seq, win, wout, cot, lo_hbm, dt_hbm, gi_hbm, go_hbm,
    xa, ca, xt, w5, wo5, wgt, kv, kvt, qs, slope, gate_t, slope_gt, dg_t, dz_t,
    at, sl, at_far, sl_far, mixed_t, stats, dm_t, z_t, z_r, g_r, dq_t, dkv_own, dkv_far, dkv_s, dkv_r,
    dpre, dx_f, dx_s, dx_r,
    ga, gb, s1, r1, s2, r2, tot, s3, r3, fr,
    go, os1, or1, os2, or2, otot, os3, or3, ofr,
    lo_out, dt_out, gi_out, go_out,
    ssem, rsem, osem,
):
    dp = lax.axis_index("dp")
    cx = lax.axis_index("ctx")
    z, xl, k = dp // 4, (dp // 2) % 2, dp % 2
    a, y = cx // 4, cx % 4
    x = a * 2 + xl

    def at_y(s):
        return {"dp": dp, "ctx": a * 4 + (y + s) % 4}

    def at_x(s):
        there = (x + s) % 4
        return {"dp": z * 4 + (there % 2) * 2 + k, "ctx": (there // 2) * 4 + y}

    def at_z(s):
        return {"dp": ((z + s) % NZ) * 4 + xl * 2 + k, "ctx": cx}

    def at_zabs(there):
        return {"dp": there * 4 + xl * 2 + k, "ctx": cx}

    def at_ctx(s):
        return {"dp": dp, "ctx": (cx + s) % 8}

    core = {"dp": z * 4 + xl * 2 + (1 - k), "ctx": cx}
    xl_mate = {"dp": z * 4 + (1 - xl) * 2 + k, "ctx": cx}
    diagonal_mate = {"dp": z * 4 + (1 - xl) * 2 + (1 - k), "ctx": cx}
    far = {"dp": dp, "ctx": (1 - a) * 4 + y}

    peers = [core, diagonal_mate, at_x(1), at_x(3)]
    peers += [at_z(s) for s in range(1, NZ)]
    peers += [at_ctx(s) for s in range(1, 8)]
    barrier = pltpu.get_barrier_semaphore()
    for peer in peers:
        pl.semaphore_signal(barrier, inc=1, device_id=peer, device_id_type=MESH)

    counter = [0]
    started = []

    def sems(n=1):
        first = counter[0]
        counter[0] += n
        return first

    def remote(src, dst, peer, s_index, r_index):
        return pltpu.make_async_remote_copy(
            src_ref=src, dst_ref=dst, send_sem=ssem.at[s_index], recv_sem=rsem.at[r_index],
            device_id=peer, device_id_type=MESH,
        )

    def send(src, dst, peer):
        i = sems()
        copy = remote(src, dst, peer, i, i)
        copy.start()
        started.append(copy)
        return copy

    def arrive(copies):
        for copy in copies:
            copy.wait_recv()

    early = pl.ds(pl.multiple_of(y * 128, 128), 128)
    late = pl.ds(pl.multiple_of((7 - y) * 128, 128), 128)

    def slots(s):
        there = (y + s) % 4
        return (
            pl.ds(pl.multiple_of(there * 128, 128), 128),
            pl.ds(pl.multiple_of((7 - there) * 128, 128), 128),
        )

    for part, block in enumerate((2, 3, 0, 1)):
        w5[z, xl, k, :, part * 128 : (part + 1) * 128] = win[
            :, pl.ds(pl.multiple_of(block * D + y * 128, 128), 128)
        ]
    wo5[z, xl, k] = wout[...]
    owner = z // 2 == y

    def normed(rows):
        v = tok[rows, :].astype(F32)
        centre = v - jnp.mean(v, axis=-1, keepdims=True)
        spread = lax.rsqrt(jnp.mean(centre * centre, axis=-1, keepdims=True) + EPS)
        return centre * spread, spread

    xa[early, :] = normed(pl.ds(0, 128))[0].astype(BF16)
    xa[late, :] = normed(pl.ds(128, 128))[0].astype(BF16)
    ca[early, :] = cot[0:128, :]
    ca[late, :] = cot[128:256, :]

    pl.semaphore_wait(barrier, len(peers))

    front, back = pl.ds(0, 256), pl.ds(256, 256)

    z_order = (4, 3, 5, 2, 6, 1, 7)

    def along_z(ref, *columns):
        part = ref.at[z, xl, k, :, *columns]
        return [send(part, part, at_z(s)) for s in z_order]

    def along_x(ref, *columns):
        part = ref.at[:, xl, k, :, *columns]
        return send(part, part, xl_mate)

    def to_core(ref, *columns):
        part = ref.at[:, :, k, :, *columns]
        return send(part, part, core)

    def onward(there):
        part = w5.at[there, xl, k, :, front]
        return [send(part, part, mate) for mate in (xl_mate, diagonal_mate, core)]

    order = (0, 1, 3, 2)
    kv_z = along_z(w5, front)
    kv_w = onward(z)
    x_y = {}
    for s in order[1:]:
        x_y[s] = [send(xa.at[early], xa.at[early], at_y(s)), send(xa.at[late], xa.at[late], at_y(s))]
    gq_z = along_z(w5, back)
    for s in (1, 7, 2, 6, 3, 5, 4):
        arrive([kv_z[z_order.index(s)]])
        kv_w += onward((z - s) % NZ)
    wo_z = along_z(wo5)
    arrive(gq_z)
    gq_w = along_x(w5, back)
    arrive(kv_w)

    def place_of(s):
        return (y - s) % 4

    def rows_of(block):
        return (
            pl.ds(pl.multiple_of(block * 128, 128), 128),
            pl.ds(pl.multiple_of((7 - block) * 128, 128), 128),
        )

    def kv_late(rows, index):
        return remote(kv.at[a, rows], kv.at[a, rows], far, index, index)

    late_first = sems(4)
    kv_x = []
    w_kv = w5[:, :, :, :, 0:256].reshape(D, 256)
    for i, s in enumerate(order):
        if s:
            arrive(x_y[s])
        if i == 1:
            c_y = []
            for t in order[1:]:
                c_y.append(send(ca.at[early], ca.at[early], at_y(t)))
                c_y.append(send(ca.at[late], ca.at[late], at_y(t)))
        first, last = rows_of(place_of(s))
        for rows in (first, last):
            pre = dot(xa[rows, :], w_kv)
            sig = sigmoid(pre)
            act = pre * sig
            kv[a, rows, :] = act.astype(BF16)
            slope[rows, 128:384] = sig + act * (1.0 - sig)
        kv_x.append(send(kv.at[a, first], kv.at[a, first], far))

        @pl.when(a == 1)
        def _():
            kv_late(last, late_first + i).start()

    arrive([gq_w])
    gq_w = to_core(w5, back)
    arrive(wo_z)
    wo_w = along_x(wo5)
    arrive([gq_w])
    wgt[...] = w5[:, :, :, :, 256:384].reshape(D, 128).T
    for i in range(4):
        rows = pl.ds(i * 256, 256)
        pre = dot(xa[rows, :], w5[:, :, :, :, 384:512].reshape(D, 128))
        sig = sigmoid(pre)
        act = pre * sig
        qs[rows, :] = act.astype(BF16)
        slope[rows, 0:128] = sig + act * (1.0 - sig)
        pre = dot(wgt[...], xa[rows, :], NT)
        sig = sigmoid(pre)
        act = pre * sig
        gate_t[:, rows] = act.astype(BF16).astype(F32)
        slope_gt[:, rows] = sig + act * (1.0 - sig)
        kvt[a, :, rows] = kv[a, rows, :].T
        xt[:, rows] = xa[rows, :].T
    mixed_t[...] = jnp.zeros_like(mixed_t)
    border = seq[0, 0]

    def tile(i):
        return pl.ds(pl.multiple_of(i * 256, 256), 256)

    def place(half, i):
        return i * 256 + half * 512 + (1 - half) * 1024 * (i // 2)

    def attend(half, kt, qt, index, diagonal):
        scores = dot(kv[half, tile(kt), 0:128], qs[tile(qt), :], NT)
        key_at = lax.broadcasted_iota(jnp.int32, (256, 256), 0) + place(half, kt)
        query_at = lax.broadcasted_iota(jnp.int32, (1, 256), 1) + place(a, qt)
        least = jnp.where(query_at >= border, border, 0)
        allowed = key_at >= least
        if diagonal:
            allowed = allowed & (key_at <= query_at)
        s = scores * SCALE
        sig = jnp.where(allowed, sigmoid(s), 0.0)
        act = s * sig
        act_b = act.astype(BF16)
        at[index] = act_b
        sl[index] = sig + act * (1.0 - sig)
        mixed_t[:, tile(qt)] += dot(kvt[half, 128:256, tile(kt)], act_b)

    for kt in range(4):
        for qt in range(kt, 4):
            attend(a, kt, qt, BASE[kt] + qt - kt, qt == kt)

    arrive([wo_w])
    wo_w = to_core(wo5)

    def far_tile(block, j):
        key_slot = block + (1 - a) * j * (7 - 2 * block)
        query_first = (1 - a + a * j) * 512
        return (
            key_slot,
            pl.ds(pl.multiple_of(key_slot * 128, 128), 128),
            pl.ds(pl.multiple_of(query_first, 512), 512),
            query_first,
        )

    def slot_place(half, slot):
        return slot * 128 + half * 512 + (1 - half) * 1024 * (slot // 4)

    for i, s in enumerate(order):
        block = place_of(s)
        first, last = rows_of(block)
        arrive([kv_x[i]])
        kvt[1 - a, :, first] = kv[1 - a, first, :].T

        @pl.when(a == 0)
        def _():
            kv_late(last, late_first + i).wait_recv()
            kvt[1, :, last] = kv[1, last, :].T

        for j in range(2):
            slot, keys, queries, query_first = far_tile(block, j)
            s_t = dot(kv[1 - a, keys, 0:128], qs[queries, :], NT) * SCALE
            key_at = lax.broadcasted_iota(jnp.int32, (128, 512), 0) + slot_place(1 - a, slot)
            query_at = lax.broadcasted_iota(jnp.int32, (1, 512), 1) + slot_place(a, query_first // 128)
            sig = jnp.where(key_at >= jnp.where(query_at >= border, border, 0), sigmoid(s_t), 0.0)
            act = s_t * sig
            act_b = act.astype(BF16)
            at_far[2 * i + j] = act_b
            sl_far[2 * i + j] = sig + act * (1.0 - sig)
            mixed_t[:, queries] += dot(kvt[1 - a, 128:256, keys], act_b)

    arrive(c_y)
    arrive([wo_w])
    head = pl.ds(pl.multiple_of(y * 2, 2), 2)
    for i in range(4):
        rows = pl.ds(i * 256, 256)
        part = dot(wo5[head].reshape(128, D), ca[rows, :], NT)
        dg_t[:, rows] = part
        dz_t[:, rows] = part * gate_t[:, rows]
    def put_sums(row, sums):
        stats[y, row : row + 1, :] = sums[:, 0:512]
        stats[y, row + 4 : row + 5, :] = sums[:, 512:1024]

    def sums_of(j, row):
        return jnp.concatenate([stats[j, row : row + 1, :], stats[j, row + 4 : row + 5, :]], axis=1)

    mixed = mixed_t[...]
    mean_h = jnp.mean(mixed, axis=0, keepdims=True)
    centred = mixed - mean_h
    dz = dz_t[...]
    put_sums(0, mean_h)
    put_sums(1, jnp.sum(centred * centred, axis=0, keepdims=True))
    put_sums(2, jnp.sum(dz, axis=0, keepdims=True))
    put_sums(3, jnp.sum(dz * centred, axis=0, keepdims=True))
    arrive([send(stats.at[y], stats.at[y], at_y(s)) for s in (1, 2, 3)])
    means = [sums_of(j, 0) for j in range(4)]
    mean = (means[0] + means[1] + means[2] + means[3]) * 0.25
    second = jnp.zeros((1, 1024), F32)
    first_dz = jnp.zeros((1, 1024), F32)
    second_dz = jnp.zeros((1, 1024), F32)
    for j in range(4):
        off = means[j] - mean
        second += sums_of(j, 1) + 128.0 * off * off
        first_dz += sums_of(j, 2)
        second_dz += sums_of(j, 3) + off * sums_of(j, 2)
    spread = lax.rsqrt(second * (1.0 / D) + EPS)
    first_dz = first_dz * (1.0 / D)
    second_dz = second_dz * (1.0 / D) * spread
    for i in range(4):
        rows = pl.ds(i * 256, 256)
        r = spread[:, i * 256 : (i + 1) * 256]
        zn = (mixed_t[:, rows] - mean[:, i * 256 : (i + 1) * 256]) * r
        z_t[:, rows] = (zn * gate_t[:, rows]).astype(BF16)
        dm_t[:, rows] = (
            r * (
                dz_t[:, rows] - first_dz[:, i * 256 : (i + 1) * 256]
                - zn * second_dz[:, i * 256 : (i + 1) * 256]
            )
        ).astype(BF16)
        dpre[rows, 256:384] = (dg_t[:, rows] * zn * slope_gt[:, rows]).astype(BF16).T

    dq_t[...] = jnp.zeros_like(dq_t)
    dkv_own[...] = jnp.zeros_like(dkv_own)
    dkv_far[...] = jnp.zeros_like(dkv_far)

    def attend_back(half, kt, qt, index, grads):
        d_attn = dot(kv[half, tile(kt), 128:256], dm_t[:, tile(qt)])
        ds = (d_attn * sl[index]).astype(BF16)
        grads[tile(kt), 128:256] += dot(at[index], dm_t[:, tile(qt)], NT)
        grads[tile(kt), 0:128] += dot(ds, qs[tile(qt), :])
        dq_t[:, tile(qt)] += dot(kvt[half, 0:128, tile(kt)], ds)

    def dkv_late(rows, index):
        return remote(dkv_s.at[rows], dkv_r.at[rows], far, index, index)

    @pl.when(a == 0)
    def _():
        dkv_r[512:1024, :] = jnp.zeros((512, 256), BF16)

    back_order = (2, 1, 3, 0)
    dkv_late_first = sems(4)
    dkv_x = []
    for i, s in enumerate(back_order):
        block = (y + s) % 4
        first, last = rows_of(block)
        index = 2 * order.index((4 - s) % 4)
        for j in range(2):
            slot, keys, queries, _ = far_tile(block, j)
            d_attn = dot(kv[1 - a, keys, 128:256], dm_t[:, queries])
            ds = (d_attn * sl_far[index + j]).astype(BF16)
            dkv_far[keys, 128:256] += dot(at_far[index + j], dm_t[:, queries], NT)
            dkv_far[keys, 0:128] += dot(ds, qs[queries, :])
            dq_t[:, queries] += dot(kvt[1 - a, 0:128, keys], ds)
        dkv_s[first, :] = dkv_far[first, :].astype(BF16)
        dkv_x.append(send(dkv_s.at[first], dkv_r.at[first], far))

        @pl.when(a == 0)
        def _():
            dkv_s[last, :] = dkv_far[last, :].astype(BF16)
            dkv_late(last, dkv_late_first + i).start()

    z_r[...] = z_t[...].T
    g_r[y, 0:128, :] = z_r[early, :]
    g_r[y, 128:256, :] = z_r[late, :]
    g_y = []
    for s in order[1:]:
        to_early, to_late = slots(s)
        g_y.append(send(z_r.at[to_early], g_r.at[y, pl.ds(0, 128)], at_y(s)))
        g_y.append(send(z_r.at[to_late], g_r.at[y, pl.ds(128, 128)], at_y(s)))
    for kt in range(4):
        for qt in range(kt, 4):
            attend_back(a, kt, qt, BASE[kt] + qt - kt, dkv_own)

    for i in range(4):
        rows = pl.ds(i * 256, 256)
        dpre[rows, 384:512] = ((dq_t[:, rows] * SCALE).T * slope[rows, 0:128]).astype(BF16)

    def grad_start(grads, first_column, n):
        for i in range(2):
            rows = pl.ds(i * 256, 256)
            part = dot(xt[rows, :], dpre[:, first_column : first_column + 256])
            grads[i * 4 : (i + 1) * 4] = part.reshape(4, 2, 2, 16, 256)
        s1[n] = grads[:, :, 1 - k].astype(BF16)
        return send(s1.at[n], r1.at[n], core)

    def grad_x(grads, n, copy):
        arrive([copy])
        grads[:, :, k] = grads[:, :, k] + r1[n].astype(F32)
        for there in range(4):
            s2[n, there] = grads[
                :, there % 2, k, :, (there // 2) * 128 : (there // 2 + 1) * 128
            ].astype(BF16)
        return [send(s2.at[n, (x + s) % 4], r2.at[n, s - 1], at_x(s)) for s in (1, 2, 3)]

    def grad_z(grads, n, copies):
        arrive(copies)
        total = grads[:, xl, k, :, pl.ds(pl.multiple_of(a * 128, 128), 128)]
        total = total + r2[n, 0].astype(F32) + r2[n, 1].astype(F32) + r2[n, 2].astype(F32)
        tot[n] = total
        s3[n] = total.astype(BF16)
        return [send(s3.at[n, (z + s) % NZ], r3.at[n, s - 1], at_z(s)) for s in z_order]

    def grad_ctx(n, copies):
        arrive(copies)
        total = tot[n, z]
        for s in range(NZ - 1):
            total = total + r3[n, s].astype(F32)
        fr[n, cx] = total
        return [send(fr.at[n, cx], fr.at[n, cx], at_ctx(s)) for s in (6, 2, 5, 7, 3, 4, 1)]

    def grad_end(n, copies):
        arrive(copies)
        for c in range(8):
            first = (n * 2 + c // 4) * D + (c % 4) * 128
            gi_out[:, first : first + 128] = fr[n, c]

    go_end_first = sems(8)
    go_end_recv = sems(2)

    def go_end(s):
        return remote(ofr.at[a], ofr.at[a], at_ctx(s), go_end_first + s, go_end_recv + a)


    dx_y = []
    w_t = w5[...].reshape(D, D)
    for i, s in enumerate(back_order):
        first, last = rows_of((y + s) % 4)
        arrive([dkv_x[i]])

        @pl.when(a == 1)
        def _():
            dkv_late(last, dkv_late_first + i).wait_recv()

        for half, rows in enumerate((first, last)):
            both = dkv_own[rows, :] + dkv_r[rows, :].astype(F32)
            dpre[rows, 0:128] = (both[:, 0:128] * SCALE * slope[rows, 128:256]).astype(BF16)
            dpre[rows, 128:256] = (both[:, 128:256] * slope[rows, 256:384]).astype(BF16)
            if s:
                dx_s[rows, :] = dot(dpre[rows, :], w_t, NT).astype(BF16)
                own = pl.ds(half * 128, 128)
                dx_y.append(send(dx_s.at[rows], dx_r.at[s - 1, own], at_y(s)))
        if i == 1:
            go[...] = dot(z_t[...], ca[...]).reshape(2, 2, 2, 16, D)
            os1[...] = go[:, :, 1 - k].astype(BF16)
            go_k = send(os1, or1, core)
        if i == 2:
            ga_k = grad_start(ga, 256, 0)
    gb_k = grad_start(gb, 0, 1)
    for half, rows in enumerate((early, late)):
        dx_f[half * 128 : (half + 1) * 128, :] = dot(dpre[rows, :], w_t, NT)
    arrive([go_k])
    go[:, :, k] = go[:, :, k] + or1[...].astype(F32)
    for there in range(4):
        os2[there] = go[:, there % 2, k, :, (there // 2) * 256 : (there // 2 + 1) * 256].astype(BF16)
    go_x = [send(os2.at[(x + s) % 4], or2.at[s - 1], at_x(s)) for s in (1, 2, 3)]
    ga_x = grad_x(ga, 0, ga_k)
    gb_x = grad_x(gb, 1, gb_k)
    arrive(go_x)
    total = go[:, xl, k, :, pl.ds(pl.multiple_of(a * 256, 256), 256)]
    total = total + or2[0].astype(F32) + or2[1].astype(F32) + or2[2].astype(F32)
    otot[...] = total
    os3[...] = total.astype(BF16)
    go_first = sems(NZ)
    go_sent = sems(2)

    def go_copy(j):
        return remote(os3.at[j], or3.at[z], at_zabs(2 * y + j), go_sent + j, go_first + z)

    for j in range(2):
        @pl.when(z != 2 * y + j)
        def _():
            go_copy(j).start()

    arrive(g_y)
    for own in (pl.ds(0, 128), pl.ds(128, 128)):
        total = tok[own, :].astype(F32)
        for h in range(4):
            total = total + dot(g_r[h, own, :], wo5[2 * h : 2 * h + 2].reshape(128, D))
        lo_out[own, :] = total.astype(BF16)
    to_hbm = [pltpu.make_async_copy(lo_out, lo_hbm, osem.at[0])]
    to_hbm[0].start()
    ga_z = grad_z(ga, 0, ga_x)
    gb_z = grad_z(gb, 1, gb_x)
    @pl.when(owner)
    def _():
        final = otot[z % 2]
        for s in range(1, NZ):
            source = (z + s) % NZ
            remote(
                os3.at[0], or3.at[source], at_z(s), go_sent, go_first + source
            ).wait_recv()
            final = final + or3[source].astype(F32)
        ofr[a] = final
        for s in range(1, 8):
            go_end(s).start()

    ga_c = grad_ctx(0, ga_z)
    arrive(dx_y)
    for i, rows in enumerate((early, late)):
        own = pl.ds(i * 128, 128)
        total = dx_f[own, :]
        for j in range(3):
            total = total + dx_r[j, own, :].astype(F32)
        xn, r = normed(own)
        first_mean = jnp.mean(total, axis=-1, keepdims=True)
        second_mean = jnp.mean(total * xn, axis=-1, keepdims=True)
        total = r * (total - first_mean - xn * second_mean) + cot[own, :].astype(F32)
        dt_out[own, :] = total.astype(BF16)
    to_hbm.append(pltpu.make_async_copy(dt_out, dt_hbm, osem.at[2]))
    to_hbm[-1].start()
    gb_c = grad_ctx(1, gb_z)
    for other in range(2):
        @pl.when(jnp.logical_or(z // 2 != y, a != other))
        def _():
            remote(
                ofr.at[other], ofr.at[other], at_ctx(1), go_end_first, go_end_recv + other
            ).wait_recv()

        go_out[:, other * 256 : (other + 1) * 256] = ofr[other]
    to_hbm.append(pltpu.make_async_copy(go_out, go_hbm, osem.at[1]))
    to_hbm[-1].start()
    grad_end(0, ga_c)
    grad_end(1, gb_c)
    to_hbm.append(pltpu.make_async_copy(gi_out, gi_hbm, osem.at[3]))
    to_hbm[-1].start()

    for copy in started:
        copy.wait_send()

    @pl.when(a == 1)
    def _():
        for i, s in enumerate(order):
            kv_late(rows_of(place_of(s))[1], late_first + i).wait_send()

    @pl.when(a == 0)
    def _():
        for i, s in enumerate(back_order):
            dkv_late(rows_of((y + s) % 4)[1], dkv_late_first + i).wait_send()

    @pl.when(owner)
    def _():
        for s in range(1, 8):
            go_end(s).wait_send()

    for j in range(2):
        @pl.when(z != 2 * y + j)
        def _():
            go_copy(j).wait_send()

    for copy in to_hbm:
        copy.wait()


N_SEMS = 200
SCRATCH = dict(
    xa=((1024, D), BF16), ca=((1024, D), BF16), xt=((D, 1024), BF16),
    w5=((NZ, 2, 2, 16, D), BF16), wo5=((NZ, 2, 2, 16, D), BF16), wgt=((128, D), BF16),
    kv=((2, 1024, 256), BF16), kvt=((2, 256, 1024), BF16), qs=((1024, 128), BF16),
    slope=((1024, 384), F32), gate_t=((128, 1024), F32), slope_gt=((128, 1024), F32),
    dg_t=((128, 1024), F32), dz_t=((128, 1024), F32),
    at=((10, 256, 256), BF16), sl=((10, 256, 256), F32),
    at_far=((8, 128, 512), BF16), sl_far=((8, 128, 512), F32), mixed_t=((128, 1024), F32),
    stats=((4, 8, 512), F32), dm_t=((128, 1024), BF16), z_t=((128, 1024), BF16),
    z_r=((1024, 128), BF16), g_r=((4, 256, 128), BF16),
    dq_t=((128, 1024), F32), dkv_own=((1024, 256), F32), dkv_far=((1024, 256), F32),
    dkv_s=((1024, 256), BF16), dkv_r=((1024, 256), BF16),
    dpre=((1024, D), BF16), dx_f=((256, D), F32), dx_s=((1024, D), BF16), dx_r=((3, 256, D), BF16),
    ga=((NZ, 2, 2, 16, 256), F32), gb=((NZ, 2, 2, 16, 256), F32),
    s1=((2, NZ, 2, 16, 256), BF16), r1=((2, NZ, 2, 16, 256), BF16),
    s2=((2, 4, NZ, 16, 128), BF16), r2=((2, 3, NZ, 16, 128), BF16), tot=((2, NZ, 16, 128), F32),
    s3=((2, NZ, 16, 128), BF16), r3=((2, NZ - 1, 16, 128), BF16), fr=((2, 8, 16, 128), F32),
    go=((2, 2, 2, 16, D), F32), os1=((2, 2, 16, D), BF16), or1=((2, 2, 16, D), BF16),
    os2=((4, 2, 16, 256), BF16), or2=((3, 2, 16, 256), BF16), otot=((2, 16, 256), F32),
    os3=((2, 16, 256), BF16), or3=((NZ, 16, 256), BF16), ofr=((2, 16, 256), F32),
    lo_out=((256, D), BF16), dt_out=((256, D), BF16), gi_out=((16, 4 * D), F32), go_out=((16, D), F32),
)


def move(*refs):
    for source, target in zip(refs[:4], refs[4:]):
        target[...] = source[...]


def body(tokens, seq_lengths, w_in, w_out, cotangent):
    vmem = pl.BlockSpec(memory_space=pltpu.VMEM)
    anywhere = pl.BlockSpec(memory_space=pl.ANY)
    outs = (
        jax.ShapeDtypeStruct((256, D), BF16),
        jax.ShapeDtypeStruct((256, D), BF16),
        jax.ShapeDtypeStruct((16, 4 * D), F32),
        jax.ShapeDtypeStruct((16, D), F32),
    )
    results = pl.pallas_call(
        kernel,
        name="hstu",
        out_shape=outs,
        in_specs=[vmem, pl.BlockSpec(memory_space=pltpu.SMEM), vmem, vmem, vmem],
        out_specs=(anywhere,) * 4,
        scratch_shapes=[pltpu.VMEM(*spec) for spec in SCRATCH.values()]
        + [pltpu.SemaphoreType.DMA((n,)) for n in (N_SEMS, N_SEMS, 4)],
        compiler_params=pltpu.CompilerParams(
            collective_id=0, has_side_effects=True, vmem_limit_bytes=56 * 2**20
        ),
    )(tokens, seq_lengths, w_in, w_out, cotangent)
    return pl.pallas_call(
        move,
        name="move",
        out_shape=outs,
        in_specs=[vmem] * 4,
        out_specs=(vmem,) * 4,
    )(*results)


def solution(mesh):
    return jax.shard_map(
        body,
        mesh=mesh,
        in_specs=(
            P(("dp", "ctx"), None),
            P("dp", None),
            P("dp", None),
            P("dp", None),
            P(("dp", "ctx"), None),
        ),
        out_specs=(P(("dp", "ctx"), None), P(("dp", "ctx"), None), P("dp", None), P("dp", None)),
        check_vma=False,
    )
```

```python
import math

import jax
import jax.numpy as jnp
from jax import lax
from jax.experimental import pallas as pl
from jax.experimental.pallas import tpu as pltpu
from jax.sharding import PartitionSpec as P

MESH = pl.DeviceIdType.MESH
F32 = jnp.float32
BF16 = jnp.bfloat16
EPS = 1e-05
NZ = 8
D = 512
H = 128
SCALE = 1.0 / math.sqrt(H)
NN = (((1,), (0,)), ((), ()))
NT = (((1,), (1,)), ((), ()))
BASE = (0, 4, 7, 9)


def dot(lhs, rhs, dims=NN):
    return lax.dot_general(lhs, rhs, dims, preferred_element_type=F32)


def sigmoid(v):
    return 0.5 * jnp.tanh(0.5 * v) + 0.5


def kernel(
    tok, seq, win, wout, cot, lo_hbm, dt_hbm, gi_hbm, go_hbm,
    xa, ca, xt, w5, wo5, wgt, kv, kvt, qs, slope, gate_t, slope_gt, dg_t, dz_t,
    at, sl, at_far, sl_far, mixed_t, stats, dm_t, z_t, z_r, g_r, dq_t, dkv_own, dkv_far, dkv_s, dkv_r,
    dpre, dx_f, dx_s, dx_r,
    ga, gb, s1, r1, s2, r2, tot, s3, r3, fr,
    go, os1, or1, os2, or2, otot, os3, or3, ofr,
    lo_out, dt_out, gi_out, go_out,
    ssem, rsem, osem,
):
    dp = lax.axis_index("dp")
    cx = lax.axis_index("ctx")
    z, xl, k = dp // 4, (dp // 2) % 2, dp % 2
    a, y = cx // 4, cx % 4
    x = a * 2 + xl

    def at_y(s):
        return {"dp": dp, "ctx": a * 4 + (y + s) % 4}

    def at_x(s):
        there = (x + s) % 4
        return {"dp": z * 4 + (there % 2) * 2 + k, "ctx": (there // 2) * 4 + y}

    def at_z(s):
        return {"dp": ((z + s) % NZ) * 4 + xl * 2 + k, "ctx": cx}

    def at_zabs(there):
        return {"dp": there * 4 + xl * 2 + k, "ctx": cx}

    def at_ctx(s):
        return {"dp": dp, "ctx": (cx + s) % 8}

    core = {"dp": z * 4 + xl * 2 + (1 - k), "ctx": cx}
    xl_mate = {"dp": z * 4 + (1 - xl) * 2 + k, "ctx": cx}
    diagonal_mate = {"dp": z * 4 + (1 - xl) * 2 + (1 - k), "ctx": cx}
    far = {"dp": dp, "ctx": (1 - a) * 4 + y}

    peers = [core, diagonal_mate, at_x(1), at_x(3)]
    peers += [at_z(s) for s in range(1, NZ)]
    peers += [at_ctx(s) for s in range(1, 8)]
    barrier = pltpu.get_barrier_semaphore()
    for peer in peers:
        pl.semaphore_signal(barrier, inc=1, device_id=peer, device_id_type=MESH)

    counter = [0]
    started = []

    def sems(n=1):
        first = counter[0]
        counter[0] += n
        return first

    def remote(src, dst, peer, s_index, r_index):
        return pltpu.make_async_remote_copy(
            src_ref=src, dst_ref=dst, send_sem=ssem.at[s_index], recv_sem=rsem.at[r_index],
            device_id=peer, device_id_type=MESH,
        )

    def send(src, dst, peer):
        i = sems()
        copy = remote(src, dst, peer, i, i)
        copy.start()
        started.append(copy)
        return copy

    def arrive(copies):
        for copy in copies:
            copy.wait_recv()

    early = pl.ds(pl.multiple_of(y * 128, 128), 128)
    late = pl.ds(pl.multiple_of((7 - y) * 128, 128), 128)

    def slots(s):
        there = (y + s) % 4
        return (
            pl.ds(pl.multiple_of(there * 128, 128), 128),
            pl.ds(pl.multiple_of((7 - there) * 128, 128), 128),
        )

    for part, block in enumerate((2, 3, 0, 1)):
        w5[z, xl, k, :, part * 128 : (part + 1) * 128] = win[
            :, pl.ds(pl.multiple_of(block * D + y * 128, 128), 128)
        ]
    wo5[z, xl, k] = wout[...]
    owner = z // 2 == y

    def normed(rows):
        v = tok[rows, :].astype(F32)
        centre = v - jnp.mean(v, axis=-1, keepdims=True)
        spread = lax.rsqrt(jnp.mean(centre * centre, axis=-1, keepdims=True) + EPS)
        return centre * spread, spread

    xa[early, :] = normed(pl.ds(0, 128))[0].astype(BF16)
    xa[late, :] = normed(pl.ds(128, 128))[0].astype(BF16)
    ca[early, :] = cot[0:128, :]
    ca[late, :] = cot[128:256, :]

    pl.semaphore_wait(barrier, len(peers))

    front, back = pl.ds(0, 256), pl.ds(256, 256)

    z_order = (4, 3, 5, 2, 6, 1, 7)

    def along_z(ref, *columns):
        part = ref.at[z, xl, k, :, *columns]
        return [send(part, part, at_z(s)) for s in z_order]

    def along_x(ref, *columns):
        part = ref.at[:, xl, k, :, *columns]
        return send(part, part, xl_mate)

    def to_core(ref, *columns):
        part = ref.at[:, :, k, :, *columns]
        return send(part, part, core)

    def onward(there):
        part = w5.at[there, xl, k, :, front]
        return [send(part, part, mate) for mate in (xl_mate, diagonal_mate, core)]

    order = (0, 1, 3, 2)
    kv_z = along_z(w5, front)
    kv_w = onward(z)
    x_y = {}
    for s in order[1:]:
        x_y[s] = [send(xa.at[early], xa.at[early], at_y(s)), send(xa.at[late], xa.at[late], at_y(s))]
    gq_z = along_z(w5, back)
    for s in (1, 7, 2, 6, 3, 5, 4):
        arrive([kv_z[z_order.index(s)]])
        kv_w += onward((z - s) % NZ)
    wo_z = along_z(wo5)
    arrive(gq_z)
    gq_w = along_x(w5, back)
    arrive(kv_w)

    def place_of(s):
        return (y - s) % 4

    def rows_of(block):
        return (
            pl.ds(pl.multiple_of(block * 128, 128), 128),
            pl.ds(pl.multiple_of((7 - block) * 128, 128), 128),
        )

    def kv_late(rows, index):
        return remote(kv.at[a, rows], kv.at[a, rows], far, index, index)

    late_first = sems(4)
    kv_x = []
    w_kv = w5[:, :, :, :, 0:256].reshape(D, 256)
    for i, s in enumerate(order):
        if s:
            arrive(x_y[s])
        if i == 1:
            c_y = []
            for t in order[1:]:
                c_y.append(send(ca.at[early], ca.at[early], at_y(t)))
                c_y.append(send(ca.at[late], ca.at[late], at_y(t)))
        first, last = rows_of(place_of(s))
        for rows in (first, last):
            pre = dot(xa[rows, :], w_kv)
            sig = sigmoid(pre)
            act = pre * sig
            kv[a, rows, :] = act.astype(BF16)
            slope[rows, 128:384] = sig + act * (1.0 - sig)
        kv_x.append(send(kv.at[a, first], kv.at[a, first], far))

        @pl.when(a == 1)
        def _():
            kv_late(last, late_first + i).start()

    arrive([gq_w])
    gq_w = to_core(w5, back)
    arrive(wo_z)
    wo_w = along_x(wo5)
    arrive([gq_w])
    wgt[...] = w5[:, :, :, :, 256:384].reshape(D, 128).T
    for i in range(4):
        rows = pl.ds(i * 256, 256)
        pre = dot(xa[rows, :], w5[:, :, :, :, 384:512].reshape(D, 128))
        sig = sigmoid(pre)
        act = pre * sig
        qs[rows, :] = act.astype(BF16)
        slope[rows, 0:128] = sig + act * (1.0 - sig)
        pre = dot(wgt[...], xa[rows, :], NT)
        sig = sigmoid(pre)
        act = pre * sig
        gate_t[:, rows] = act.astype(BF16).astype(F32)
        slope_gt[:, rows] = sig + act * (1.0 - sig)
        kvt[a, :, rows] = kv[a, rows, :].T
        xt[:, rows] = xa[rows, :].T
    mixed_t[...] = jnp.zeros_like(mixed_t)
    border = seq[0, 0]

    def tile(i):
        return pl.ds(pl.multiple_of(i * 256, 256), 256)

    def place(half, i):
        return i * 256 + half * 512 + (1 - half) * 1024 * (i // 2)

    def attend(half, kt, qt, index, diagonal):
        scores = dot(kv[half, tile(kt), 0:128], qs[tile(qt), :], NT)
        key_at = lax.broadcasted_iota(jnp.int32, (256, 256), 0) + place(half, kt)
        query_at = lax.broadcasted_iota(jnp.int32, (1, 256), 1) + place(a, qt)
        least = jnp.where(query_at >= border, border, 0)
        allowed = key_at >= least
        if diagonal:
            allowed = allowed & (key_at <= query_at)
        s = scores * SCALE
        sig = jnp.where(allowed, sigmoid(s), 0.0)
        act = s * sig
        act_b = act.astype(BF16)
        at[index] = act_b
        sl[index] = sig + act * (1.0 - sig)
        mixed_t[:, tile(qt)] += dot(kvt[half, 128:256, tile(kt)], act_b)

    for kt in range(4):
        for qt in range(kt, 4):
            attend(a, kt, qt, BASE[kt] + qt - kt, qt == kt)

    arrive([wo_w])
    wo_w = to_core(wo5)

    def far_tile(block, j):
        key_slot = block + (1 - a) * j * (7 - 2 * block)
        query_first = (1 - a + a * j) * 512
        return (
            key_slot,
            pl.ds(pl.multiple_of(key_slot * 128, 128), 128),
            pl.ds(pl.multiple_of(query_first, 512), 512),
            query_first,
        )

    def slot_place(half, slot):
        return slot * 128 + half * 512 + (1 - half) * 1024 * (slot // 4)

    for i, s in enumerate(order):
        block = place_of(s)
        first, last = rows_of(block)
        arrive([kv_x[i]])
        kvt[1 - a, :, first] = kv[1 - a, first, :].T

        @pl.when(a == 0)
        def _():
            kv_late(last, late_first + i).wait_recv()
            kvt[1, :, last] = kv[1, last, :].T

        for j in range(2):
            slot, keys, queries, query_first = far_tile(block, j)
            s_t = dot(kv[1 - a, keys, 0:128], qs[queries, :], NT) * SCALE
            key_at = lax.broadcasted_iota(jnp.int32, (128, 512), 0) + slot_place(1 - a, slot)
            query_at = lax.broadcasted_iota(jnp.int32, (1, 512), 1) + slot_place(a, query_first // 128)
            sig = jnp.where(key_at >= jnp.where(query_at >= border, border, 0), sigmoid(s_t), 0.0)
            act = s_t * sig
            act_b = act.astype(BF16)
            at_far[2 * i + j] = act_b
            sl_far[2 * i + j] = sig + act * (1.0 - sig)
            mixed_t[:, queries] += dot(kvt[1 - a, 128:256, keys], act_b)

    arrive(c_y)
    arrive([wo_w])
    head = pl.ds(pl.multiple_of(y * 2, 2), 2)
    for i in range(4):
        rows = pl.ds(i * 256, 256)
        part = dot(wo5[head].reshape(128, D), ca[rows, :], NT)
        dg_t[:, rows] = part
        dz_t[:, rows] = part * gate_t[:, rows]
    def put_sums(row, sums):
        stats[y, row : row + 1, :] = sums[:, 0:512]
        stats[y, row + 4 : row + 5, :] = sums[:, 512:1024]

    def sums_of(j, row):
        return jnp.concatenate([stats[j, row : row + 1, :], stats[j, row + 4 : row + 5, :]], axis=1)

    mixed = mixed_t[...]
    mean_h = jnp.mean(mixed, axis=0, keepdims=True)
    centred = mixed - mean_h
    dz = dz_t[...]
    put_sums(0, mean_h)
    put_sums(1, jnp.sum(centred * centred, axis=0, keepdims=True))
    put_sums(2, jnp.sum(dz, axis=0, keepdims=True))
    put_sums(3, jnp.sum(dz * centred, axis=0, keepdims=True))
    arrive([send(stats.at[y], stats.at[y], at_y(s)) for s in (1, 2, 3)])
    means = [sums_of(j, 0) for j in range(4)]
    mean = (means[0] + means[1] + means[2] + means[3]) * 0.25
    second = jnp.zeros((1, 1024), F32)
    first_dz = jnp.zeros((1, 1024), F32)
    second_dz = jnp.zeros((1, 1024), F32)
    for j in range(4):
        off = means[j] - mean
        second += sums_of(j, 1) + 128.0 * off * off
        first_dz += sums_of(j, 2)
        second_dz += sums_of(j, 3) + off * sums_of(j, 2)
    spread = lax.rsqrt(second * (1.0 / D) + EPS)
    first_dz = first_dz * (1.0 / D)
    second_dz = second_dz * (1.0 / D) * spread
    for i in range(4):
        rows = pl.ds(i * 256, 256)
        r = spread[:, i * 256 : (i + 1) * 256]
        zn = (mixed_t[:, rows] - mean[:, i * 256 : (i + 1) * 256]) * r
        z_t[:, rows] = (zn * gate_t[:, rows]).astype(BF16)
        dm_t[:, rows] = (
            r * (
                dz_t[:, rows] - first_dz[:, i * 256 : (i + 1) * 256]
                - zn * second_dz[:, i * 256 : (i + 1) * 256]
            )
        ).astype(BF16)
        dg_t[:, rows] = dg_t[:, rows] * zn

    dq_t[...] = jnp.zeros_like(dq_t)
    dkv_own[...] = jnp.zeros_like(dkv_own)
    dkv_far[...] = jnp.zeros_like(dkv_far)

    def attend_back(half, kt, qt, index, grads):
        d_attn = dot(kv[half, tile(kt), 128:256], dm_t[:, tile(qt)])
        ds = (d_attn * sl[index]).astype(BF16)
        grads[tile(kt), 128:256] += dot(at[index], dm_t[:, tile(qt)], NT)
        grads[tile(kt), 0:128] += dot(ds, qs[tile(qt), :])
        dq_t[:, tile(qt)] += dot(kvt[half, 0:128, tile(kt)], ds)

    def dkv_late(rows, index):
        return remote(dkv_s.at[rows], dkv_r.at[rows], far, index, index)

    @pl.when(a == 0)
    def _():
        dkv_r[512:1024, :] = jnp.zeros((512, 256), BF16)

    back_order = (2, 1, 3, 0)
    dkv_late_first = sems(4)
    dkv_x = []
    for i, s in enumerate(back_order):
        block = (y + s) % 4
        first, last = rows_of(block)
        index = 2 * order.index((4 - s) % 4)
        for j in range(2):
            slot, keys, queries, _ = far_tile(block, j)
            d_attn = dot(kv[1 - a, keys, 128:256], dm_t[:, queries])
            ds = (d_attn * sl_far[index + j]).astype(BF16)
            dkv_far[keys, 128:256] += dot(at_far[index + j], dm_t[:, queries], NT)
            dkv_far[keys, 0:128] += dot(ds, qs[queries, :])
            dq_t[:, queries] += dot(kvt[1 - a, 0:128, keys], ds)
        dkv_s[first, :] = dkv_far[first, :].astype(BF16)
        dkv_x.append(send(dkv_s.at[first], dkv_r.at[first], far))

        @pl.when(a == 0)
        def _():
            dkv_s[last, :] = dkv_far[last, :].astype(BF16)
            dkv_late(last, dkv_late_first + i).start()

    z_r[...] = z_t[...].T
    g_r[y, 0:128, :] = z_r[early, :]
    g_r[y, 128:256, :] = z_r[late, :]
    g_y = []
    for s in order[1:]:
        to_early, to_late = slots(s)
        g_y.append(send(z_r.at[to_early], g_r.at[y, pl.ds(0, 128)], at_y(s)))
        g_y.append(send(z_r.at[to_late], g_r.at[y, pl.ds(128, 128)], at_y(s)))
    for i in range(4):
        rows = pl.ds(i * 256, 256)
        dpre[rows, 256:384] = (dg_t[:, rows] * slope_gt[:, rows]).astype(BF16).T

    for kt in range(4):
        for qt in range(kt, 4):
            attend_back(a, kt, qt, BASE[kt] + qt - kt, dkv_own)

    for i in range(4):
        rows = pl.ds(i * 256, 256)
        dpre[rows, 384:512] = ((dq_t[:, rows] * SCALE).T * slope[rows, 0:128]).astype(BF16)

    def grad_start(grads, first_column, n):
        for i in range(2):
            rows = pl.ds(i * 256, 256)
            part = dot(xt[rows, :], dpre[:, first_column : first_column + 256])
            grads[i * 4 : (i + 1) * 4] = part.reshape(4, 2, 2, 16, 256)
        s1[n] = grads[:, :, 1 - k].astype(BF16)
        return send(s1.at[n], r1.at[n], core)

    def grad_x(grads, n, copy):
        arrive([copy])
        grads[:, :, k] = grads[:, :, k] + r1[n].astype(F32)
        for there in range(4):
            s2[n, there] = grads[
                :, there % 2, k, :, (there // 2) * 128 : (there // 2 + 1) * 128
            ].astype(BF16)
        return [send(s2.at[n, (x + s) % 4], r2.at[n, s - 1], at_x(s)) for s in (1, 2, 3)]

    def grad_z(grads, n, copies):
        arrive(copies)
        total = grads[:, xl, k, :, pl.ds(pl.multiple_of(a * 128, 128), 128)]
        total = total + r2[n, 0].astype(F32) + r2[n, 1].astype(F32) + r2[n, 2].astype(F32)
        tot[n] = total
        s3[n] = total.astype(BF16)
        return [send(s3.at[n, (z + s) % NZ], r3.at[n, s - 1], at_z(s)) for s in z_order]

    def grad_ctx(n, copies):
        arrive(copies)
        total = tot[n, z]
        for s in range(NZ - 1):
            total = total + r3[n, s].astype(F32)
        fr[n, cx] = total
        return [send(fr.at[n, cx], fr.at[n, cx], at_ctx(s)) for s in (6, 2, 5, 7, 3, 4, 1)]

    def grad_end(n, copies):
        arrive(copies)
        for c in range(8):
            first = (n * 2 + c // 4) * D + (c % 4) * 128
            gi_out[:, first : first + 128] = fr[n, c]

    go_end_first = sems(8)
    go_end_recv = sems(2)

    def go_end(s):
        return remote(ofr.at[a], ofr.at[a], at_ctx(s), go_end_first + s, go_end_recv + a)


    dx_y = []
    w_t = w5[...].reshape(D, D)
    for i, s in enumerate(back_order):
        first, last = rows_of((y + s) % 4)
        arrive([dkv_x[i]])

        @pl.when(a == 1)
        def _():
            dkv_late(last, dkv_late_first + i).wait_recv()

        for half, rows in enumerate((first, last)):
            both = dkv_own[rows, :] + dkv_r[rows, :].astype(F32)
            dpre[rows, 0:128] = (both[:, 0:128] * SCALE * slope[rows, 128:256]).astype(BF16)
            dpre[rows, 128:256] = (both[:, 128:256] * slope[rows, 256:384]).astype(BF16)
            if s:
                dx_s[rows, :] = dot(dpre[rows, :], w_t, NT).astype(BF16)
                own = pl.ds(half * 128, 128)
                dx_y.append(send(dx_s.at[rows], dx_r.at[s - 1, own], at_y(s)))
        if i == 1:
            go[...] = dot(z_t[...], ca[...]).reshape(2, 2, 2, 16, D)
            os1[...] = go[:, :, 1 - k].astype(BF16)
            go_k = send(os1, or1, core)
        if i == 2:
            ga_k = grad_start(ga, 256, 0)
    gb_k = grad_start(gb, 0, 1)
    for half, rows in enumerate((early, late)):
        dx_f[half * 128 : (half + 1) * 128, :] = dot(dpre[rows, :], w_t, NT)
    arrive([go_k])
    go[:, :, k] = go[:, :, k] + or1[...].astype(F32)
    for there in range(4):
        os2[there] = go[:, there % 2, k, :, (there // 2) * 256 : (there // 2 + 1) * 256].astype(BF16)
    go_x = [send(os2.at[(x + s) % 4], or2.at[s - 1], at_x(s)) for s in (1, 2, 3)]
    ga_x = grad_x(ga, 0, ga_k)
    gb_x = grad_x(gb, 1, gb_k)
    arrive(go_x)
    total = go[:, xl, k, :, pl.ds(pl.multiple_of(a * 256, 256), 256)]
    total = total + or2[0].astype(F32) + or2[1].astype(F32) + or2[2].astype(F32)
    otot[...] = total
    os3[...] = total.astype(BF16)
    go_first = sems(NZ)
    go_sent = sems(2)

    def go_copy(j):
        return remote(os3.at[j], or3.at[z], at_zabs(2 * y + j), go_sent + j, go_first + z)

    for j in range(2):
        @pl.when(z != 2 * y + j)
        def _():
            go_copy(j).start()

    arrive(g_y)
    for own in (pl.ds(0, 128), pl.ds(128, 128)):
        total = tok[own, :].astype(F32)
        for h in range(4):
            total = total + dot(g_r[h, own, :], wo5[2 * h : 2 * h + 2].reshape(128, D))
        lo_out[own, :] = total.astype(BF16)
    to_hbm = [pltpu.make_async_copy(lo_out, lo_hbm, osem.at[0])]
    to_hbm[0].start()
    ga_z = grad_z(ga, 0, ga_x)
    gb_z = grad_z(gb, 1, gb_x)
    @pl.when(owner)
    def _():
        final = otot[z % 2]
        for s in range(1, NZ):
            source = (z + s) % NZ
            remote(
                os3.at[0], or3.at[source], at_z(s), go_sent, go_first + source
            ).wait_recv()
            final = final + or3[source].astype(F32)
        ofr[a] = final
        for s in range(1, 8):
            go_end(s).start()

    ga_c = grad_ctx(0, ga_z)
    arrive(dx_y)
    for i, rows in enumerate((early, late)):
        own = pl.ds(i * 128, 128)
        total = dx_f[own, :]
        for j in range(3):
            total = total + dx_r[j, own, :].astype(F32)
        xn, r = normed(own)
        first_mean = jnp.mean(total, axis=-1, keepdims=True)
        second_mean = jnp.mean(total * xn, axis=-1, keepdims=True)
        total = r * (total - first_mean - xn * second_mean) + cot[own, :].astype(F32)
        dt_out[own, :] = total.astype(BF16)
    to_hbm.append(pltpu.make_async_copy(dt_out, dt_hbm, osem.at[2]))
    to_hbm[-1].start()
    gb_c = grad_ctx(1, gb_z)
    for other in range(2):
        @pl.when(jnp.logical_or(z // 2 != y, a != other))
        def _():
            remote(
                ofr.at[other], ofr.at[other], at_ctx(1), go_end_first, go_end_recv + other
            ).wait_recv()

        go_out[:, other * 256 : (other + 1) * 256] = ofr[other]
    to_hbm.append(pltpu.make_async_copy(go_out, go_hbm, osem.at[1]))
    to_hbm[-1].start()
    grad_end(0, ga_c)
    grad_end(1, gb_c)
    to_hbm.append(pltpu.make_async_copy(gi_out, gi_hbm, osem.at[3]))
    to_hbm[-1].start()

    for copy in started:
        copy.wait_send()

    @pl.when(a == 1)
    def _():
        for i, s in enumerate(order):
            kv_late(rows_of(place_of(s))[1], late_first + i).wait_send()

    @pl.when(a == 0)
    def _():
        for i, s in enumerate(back_order):
            dkv_late(rows_of((y + s) % 4)[1], dkv_late_first + i).wait_send()

    @pl.when(owner)
    def _():
        for s in range(1, 8):
            go_end(s).wait_send()

    for j in range(2):
        @pl.when(z != 2 * y + j)
        def _():
            go_copy(j).wait_send()

    for copy in to_hbm:
        copy.wait()


N_SEMS = 200
SCRATCH = dict(
    xa=((1024, D), BF16), ca=((1024, D), BF16), xt=((D, 1024), BF16),
    w5=((NZ, 2, 2, 16, D), BF16), wo5=((NZ, 2, 2, 16, D), BF16), wgt=((128, D), BF16),
    kv=((2, 1024, 256), BF16), kvt=((2, 256, 1024), BF16), qs=((1024, 128), BF16),
    slope=((1024, 384), F32), gate_t=((128, 1024), F32), slope_gt=((128, 1024), F32),
    dg_t=((128, 1024), F32), dz_t=((128, 1024), F32),
    at=((10, 256, 256), BF16), sl=((10, 256, 256), F32),
    at_far=((8, 128, 512), BF16), sl_far=((8, 128, 512), F32), mixed_t=((128, 1024), F32),
    stats=((4, 8, 512), F32), dm_t=((128, 1024), BF16), z_t=((128, 1024), BF16),
    z_r=((1024, 128), BF16), g_r=((4, 256, 128), BF16),
    dq_t=((128, 1024), F32), dkv_own=((1024, 256), F32), dkv_far=((1024, 256), F32),
    dkv_s=((1024, 256), BF16), dkv_r=((1024, 256), BF16),
    dpre=((1024, D), BF16), dx_f=((256, D), F32), dx_s=((1024, D), BF16), dx_r=((3, 256, D), BF16),
    ga=((NZ, 2, 2, 16, 256), F32), gb=((NZ, 2, 2, 16, 256), F32),
    s1=((2, NZ, 2, 16, 256), BF16), r1=((2, NZ, 2, 16, 256), BF16),
    s2=((2, 4, NZ, 16, 128), BF16), r2=((2, 3, NZ, 16, 128), BF16), tot=((2, NZ, 16, 128), F32),
    s3=((2, NZ, 16, 128), BF16), r3=((2, NZ - 1, 16, 128), BF16), fr=((2, 8, 16, 128), F32),
    go=((2, 2, 2, 16, D), F32), os1=((2, 2, 16, D), BF16), or1=((2, 2, 16, D), BF16),
    os2=((4, 2, 16, 256), BF16), or2=((3, 2, 16, 256), BF16), otot=((2, 16, 256), F32),
    os3=((2, 16, 256), BF16), or3=((NZ, 16, 256), BF16), ofr=((2, 16, 256), F32),
    lo_out=((256, D), BF16), dt_out=((256, D), BF16), gi_out=((16, 4 * D), F32), go_out=((16, D), F32),
)


def move(*refs):
    for source, target in zip(refs[:4], refs[4:]):
        target[...] = source[...]


def body(tokens, seq_lengths, w_in, w_out, cotangent):
    vmem = pl.BlockSpec(memory_space=pltpu.VMEM)
    anywhere = pl.BlockSpec(memory_space=pl.ANY)
    outs = (
        jax.ShapeDtypeStruct((256, D), BF16),
        jax.ShapeDtypeStruct((256, D), BF16),
        jax.ShapeDtypeStruct((16, 4 * D), F32),
        jax.ShapeDtypeStruct((16, D), F32),
    )
    results = pl.pallas_call(
        kernel,
        name="hstu",
        out_shape=outs,
        in_specs=[vmem, pl.BlockSpec(memory_space=pltpu.SMEM), vmem, vmem, vmem],
        out_specs=(anywhere,) * 4,
        scratch_shapes=[pltpu.VMEM(*spec) for spec in SCRATCH.values()]
        + [pltpu.SemaphoreType.DMA((n,)) for n in (N_SEMS, N_SEMS, 4)],
        compiler_params=pltpu.CompilerParams(
            collective_id=0, has_side_effects=True, vmem_limit_bytes=56 * 2**20
        ),
    )(tokens, seq_lengths, w_in, w_out, cotangent)
    return pl.pallas_call(
        move,
        name="move",
        out_shape=outs,
        in_specs=[vmem] * 4,
        out_specs=(vmem,) * 4,
    )(*results)


def solution(mesh):
    return jax.shard_map(
        body,
        mesh=mesh,
        in_specs=(
            P(("dp", "ctx"), None),
            P("dp", None),
            P("dp", None),
            P("dp", None),
            P(("dp", "ctx"), None),
        ),
        out_specs=(P(("dp", "ctx"), None), P(("dp", "ctx"), None), P("dp", None), P("dp", None)),
        check_vma=False,
    )
```
